512 devices in a mesh: lat: 64 (over x, y, z_hi), lev: 8 (over z_lo, core).
Axes of the slice: x: 4, y: 4, z: 16 (z_hi: 4, z_lo: 4; z = z_hi * 4 + z_lo), core: 2. Of those that a mesh axis runs over, the one named last changes fastest.
Arguments:
- tracers: float32 [8, 8, 768, 1152], P(None, 'lev', 'lat'), may hold values from -6 to 6
- thickness: float32 [8, 768, 1152], P('lev', 'lat'), may hold values from 0.85 to 1.15
- courant_x: float32 [8, 768, 1152], P('lev', 'lat'), may hold values from -0.08 to 0.08
- courant_y: float32 [8, 768, 1152], P('lev', 'lat'), may hold values from -0.08 to 0.08
- level_weights: float32 [8], replicated, may hold values from 0.5 to 2
Outputs:
- remapped: float32 [8, 8, 768, 1152], P(None, None, 'lat', 'lev')
- column_mass: float32 [768, 1152], P('lat', 'lev')
The draws below stay inside these ranges and needn't reach their ends.
All inputs are finite; a program needn't handle non-finite values.
Results may differ from the reference program's by a relative error of at most 0.0003.
Values sent between devices are 32-bit elements; how exact they have to be, the bound alone decides.
No kernel may reach another device: no remote copies, remote signals or barrier semaphores. Data moves between devices by JAX's collectives and lax.ppermute only.
A program may use at most 128 MiB of HBM per device.

```python
import math
import jax
import jax.numpy as jnp
from jax import lax

NLON = 1152
NTRACER = 8
NLAT = 768
NLEV = 8


def block_scale(rng, dims, shards, low, largest):
    def one(position, parts):
        steps = jax.random.uniform(jax.random.fold_in(jax.random.fold_in(rng, 6), position), (parts,), jnp.float32, low / len(shards), largest / len(shards))
        return jnp.repeat(jnp.exp(steps), dims[position] // parts).reshape((-1,) + (1,) * (len(dims) - position - 1))

    loudness = one(*shards[0])
    for cut in shards[1:]:
        loudness = loudness * one(*cut)
    return loudness


def bell_draw(rng, extent, deviation, limit, pieces=(), dtype=jnp.bfloat16):
    entries = deviation * jax.random.normal(rng, extent, jnp.float32)
    if pieces:
        entries = entries * block_scale(rng, extent, pieces, -0.22, 0.18)
    return jnp.clip(entries, -limit, limit).astype(dtype)


def setup_inputs(seed: int = 0) -> dict:
    arg_keys = jax.random.split(jax.random.key(seed), 6)
    return {
        "tracers": bell_draw(arg_keys[0], (NTRACER, NLEV, NLAT, NLON), 1.0, 6.0, ((1, 8), (2, 64)), jnp.float32),
        "thickness": jnp.clip(0.85 + 0.29999995 * jax.random.uniform(arg_keys[1], (NLEV, NLAT, NLON), jnp.float32) ** block_scale(arg_keys[1], (NLEV, NLAT, NLON), ((0, 8), (1, 64)), -0.2, 0.2), 0.85, 1.15),
        "courant_x": jnp.clip(jax.random.uniform(arg_keys[2], (NLEV, NLAT, NLON), jnp.float32, -0.08, 0.08) * block_scale(arg_keys[2], (NLEV, NLAT, NLON), ((0, 8), (1, 64)), -0.4, 0.0), -0.08, 0.08),
        "courant_y": jnp.clip(jax.random.uniform(arg_keys[3], (NLEV, NLAT, NLON), jnp.float32, -0.08, 0.08) * block_scale(arg_keys[3], (NLEV, NLAT, NLON), ((0, 8), (1, 64)), -0.4, 0.0), -0.08, 0.08),
        "level_weights": jnp.clip(jnp.exp(jax.random.uniform(arg_keys[4], (NLEV,), jnp.float32, math.log(0.5), math.log(2.0))), 0.5, 2.0),
    }


def swept_average(left_cell, right_cell, left_lo, middle, right_hi, courant):
    left_slope = middle - left_lo
    left_curve = 6.0 * (left_cell - 0.5 * (left_lo + middle))
    forward = middle - 0.5 * courant * (left_slope - (1.0 - 2.0 * courant / 3.0) * left_curve)
    reverse_c = -courant
    right_slope = right_hi - middle
    right_curve = 6.0 * (right_cell - 0.5 * (middle + right_hi))
    backward = middle + 0.5 * reverse_c * (right_slope + (1.0 - 2.0 * reverse_c / 3.0) * right_curve)
    return jnp.where(courant > 0.0, forward, backward)


def face_values(extended, courant, axis_dim):
    face_count = extended.shape[axis_dim] - 5

    def take_rows(offset, length):
        return lax.slice_in_dim(extended, offset, offset + length, axis=axis_dim)

    edge_values = (7.0 / 12.0) * (take_rows(1, face_count + 2) + take_rows(2, face_count + 2)) - (1.0 / 12.0) * (take_rows(0, face_count + 2) + take_rows(3, face_count + 2))

    def edge_run(offset):
        return lax.slice_in_dim(edge_values, offset, offset + face_count, axis=axis_dim)

    return swept_average(take_rows(2, face_count), take_rows(3, face_count), edge_run(0), edge_run(1), edge_run(2), courant)


def remap_row(ratio_row, thick_row, shares):
    column_total = jnp.sum(thick_row, axis=0)
    upper_edge = jnp.cumsum(thick_row, axis=0)
    lower_edge = upper_edge - thick_row
    target = shares[:, None] * column_total[None]
    target_upper = jnp.cumsum(target, axis=0)
    target_lower = target_upper - target
    intersection = jnp.maximum(0.0, jnp.minimum(upper_edge[:, None], target_upper[None]) - jnp.maximum(lower_edge[:, None], target_lower[None]))
    moved_mass = jnp.einsum("tic,ikc->tkc", ratio_row, intersection, precision=lax.Precision.HIGHEST)
    return moved_mass / target[None]


def reference(tracers, thickness, courant_x, courant_y, level_weights):
    row_ids = jnp.arange(NLAT).astype(jnp.float32)
    centre = jnp.sin(math.pi * (row_ids + 0.5) / NLAT)
    face_cos = jnp.sin(math.pi * jnp.arange(NLAT + 1).astype(jnp.float32) / NLAT)
    cx_faces = jnp.concatenate([courant_x, courant_x[:, :, :1]], axis=2)
    cy_faces = jnp.concatenate([courant_y, jnp.zeros_like(courant_y[:, :1])], axis=1)

    def wrap_lon(field):
        return jnp.concatenate([field[..., -3:], field, field[..., :3]], axis=-1)

    def pad_lat(field):
        return jnp.pad(field, ((0, 0), (3, 3), (0, 0)))

    def div_x(flux):
        return flux[:, :, 1:] - flux[:, :, :-1]

    def div_y(flux):
        return (flux[:, 1:] - flux[:, :-1]) / centre[None, :, None]

    mass_x = cx_faces * face_values(wrap_lon(thickness), cx_faces, 2)
    mass_y = cy_faces * face_values(pad_lat(thickness), cy_faces, 1) * face_cos[None, :, None]
    new_thick = thickness - div_x(mass_x) - div_y(mass_y)
    wavenumber = jnp.arange(NLON // 2 + 1)
    sines = jnp.sin(math.pi * wavenumber.astype(jnp.float32) / NLON)
    safe_sq = jnp.where(wavenumber == 0, 1.0, sines * sines)
    damping = jnp.where(wavenumber[None] == 0, 1.0, jnp.minimum(1.0, 4.0 * centre[:, None] ** 2 / safe_sq[None]))

    def one_tracer(tracer):
        zonal = div_x(mass_x * face_values(wrap_lon(tracer), cx_faces, 2))
        spectrum = jnp.fft.rfft(zonal, axis=-1) * damping[None]
        zonal = jnp.fft.irfft(spectrum, n=NLON, axis=-1).astype(jnp.float32)
        merid = div_y(mass_y * face_values(pad_lat(tracer), cy_faces, 1))
        return (thickness * tracer - zonal - merid) / new_thick

    ratios = lax.map(one_tracer, tracers)
    column_mass = jnp.sum(new_thick, axis=0)
    shares = level_weights / jnp.sum(level_weights)

    def per_row(pair):
        return remap_row(pair[0], pair[1], shares)

    moved = lax.map(per_row, (jnp.moveaxis(ratios, 2, 0), jnp.moveaxis(new_thick, 1, 0)))
    return jnp.moveaxis(moved, 0, 2), column_mass
```

```python
import math

import jax
import jax.numpy as jnp
import ml_dtypes
import numpy as np
from jax import lax
from jax.experimental import pallas as pl
from jax.experimental.pallas import tpu as pltpu
from jax.sharding import PartitionSpec as P

NT = 8
NLEV = 8
NLAT = 768
NLON = 1152
ROWS = 12
LANES = 128
CHUNKS = NLON // LANES
PIECE = NLON // NLEV
TAIL = PIECE - LANES
HALO = 3
INNER = tuple(range(HALO, ROWS - HALO))
OUTER = tuple(range(HALO)) + tuple(range(ROWS - HALO, ROWS))
HALF = ROWS // 2
MSG = 64
UP_ROWS = 248
DOWN_ROWS = 256
F32 = jnp.float32
BF16 = jnp.bfloat16


def vmem():
    return pl.BlockSpec(memory_space=pltpu.VMEM)


def params(mib):
    return pltpu.CompilerParams(vmem_limit_bytes=mib * 1024 * 1024)


def shifted(x, d):
    return x if d == 0 else pltpu.roll(x, (-d) % NLON, 1)


def face_coefs(courant):
    m = jnp.abs(courant)
    k = m * (3.0 - 2.0 * m)
    return 1.0 - 0.5 * (m + k), k, 0.5 * (m - k), courant > 0.0


def flux_stencil(mass, n, k, w, positive):
    zero = jnp.zeros_like(mass)
    a, b, c = mass * n, mass * k, mass * w
    bp, cp = jnp.where(positive, b, zero), jnp.where(positive, c, zero)
    bm, cm = b - bp, c - cp
    s, t = 7.0 / 12.0, 1.0 / 12.0
    return (
        -t * cp,
        s * cp - t * a,
        s * (a + cp) - t * cm + bp,
        s * (a + cm) - t * cp + bm,
        s * cm - t * a,
        -t * cm,
    )


def divergence_stencil(faces, ahead):
    nxt = [ahead(f) for f in faces]
    return (
        [-faces[0]] + [nxt[i] - faces[i + 1] for i in range(5)] + [nxt[5]]
    )


def meridional(band, hx, cy, e_scr, base, store):
    first = (band * ROWS).astype(F32)
    ids = first + lax.broadcasted_iota(jnp.int32, (16, LANES), 0).astype(F32)
    centre = jnp.sin(math.pi * (ids + 0.5) / NLAT)[:, :1]
    face_cos = jnp.sin(math.pi * ids / NLAT)[:, :1]
    e_scr[0:16] = (7.0 / 12.0) * (hx[1:17] + hx[2:18]) - (1.0 / 12.0) * (hx[0:16] + hx[3:19])
    e_scr[16:24] = jnp.zeros((8, NLON), F32)
    c = cy[...]
    n, k, w, positive = face_coefs(c)
    cell = jnp.where(positive, hx[2:18], hx[3:19])
    far = jnp.where(positive, e_scr[0:16], e_scr[2:18])
    mass = c * face_cos * (n * e_scr[1:17] + k * cell + w * far)
    faces = flux_stencil(mass, n, k, w, positive)

    def ahead(x):
        return pltpu.roll(x, 15, 0)

    stencil = divergence_stencil(faces, ahead)
    per_centre = 1.0 / centre
    new_thick = base - (ahead(mass) - mass) * per_centre
    inverse = 1.0 / new_thick
    scale = inverse * per_centre
    for d in range(7):
        weight = -stencil[d] * scale
        if d == 3:
            weight = weight + hx[3:19] * inverse
        store[d] = weight
    store[7] = -inverse
    return new_thick


def row_of(ref, index, row):
    return jnp.broadcast_to(ref[index, row : row + 1, :], (NT, NLON))


def lane_ids(rows=NT):
    return lax.broadcasted_iota(jnp.int32, (rows, LANES), 1)


def turn(x, amount):
    amount %= LANES
    return x if amount == 0 else pltpu.roll(x, amount, 1)


def window(lanes, low, high, dest):
    if dest == 0:
        return low
    keep = lanes < LANES - TAIL * dest
    return jnp.where(keep, turn(low, -TAIL * dest), turn(high, -TAIL * dest))


def pack_message(rows, ratio_row, new_thick, msg):
    lanes = lane_ids()
    tails = [jnp.zeros((NT, LANES), F32)] * NLEV
    for v, r in enumerate(rows):
        ratio = ratio_row(r)
        part = [ratio[:, LANES * c : LANES * (c + 1)] for c in range(CHUNKS)]
        here = (lanes >= TAIL * v) & (lanes < TAIL * (v + 1))
        for dest in range(NLEV):
            msg[dest, 8 * v : 8 * v + 8, :] = window(lanes, part[dest], part[dest + 1], dest)
            tails[dest] = jnp.where(here, turn(part[dest + 1], TAIL * (v - dest)), tails[dest])
    for dest in range(NLEV):
        msg[dest, 8 * HALF : 8 * HALF + 8, :] = tails[dest]
    lanes16 = lane_ids(16)
    wide = lane_ids(1)
    base = 8 * HALF + 8
    for dest in range(NLEV):
        low = new_thick[:, LANES * dest : LANES * (dest + 1)]
        high = new_thick[:, LANES * (dest + 1) : LANES * (dest + 2)]
        main = window(lanes16, low, high, dest)
        last = jnp.ones((1, LANES), F32)
        for v, r in enumerate(rows):
            msg[dest, base + v : base + v + 1, :] = main[r : r + 1]
            here = (wide >= TAIL * v) & (wide < TAIL * (v + 1))
            last = jnp.where(here, turn(high[r : r + 1], TAIL * (v - dest)), last)
        msg[dest, base + HALF : base + HALF + 1, :] = last
        msg[dest, base + HALF + 1 : base + HALF + 2, :] = jnp.ones((1, LANES), F32)


def edge_kernel(q_ref, h_ref, cy_ref, up_ref, down_ref):
    for ref, first in ((up_ref, ROWS - HALO), (down_ref, 0)):
        for i in range(HALO):
            row = q_ref[:, 0, first + i, :]
            for c in range(CHUNKS):
                at = 8 * (CHUNKS * i + c)
                ref[at : at + 8, :] = row[:, LANES * c : LANES * (c + 1)]
        for c in range(CHUNKS):
            at = 8 * CHUNKS * HALO + HALO * c
            ref[at : at + HALO, :] = h_ref[0, first : first + HALO, LANES * c : LANES * (c + 1)]
    for c in range(CHUNKS):
        at = (8 * HALO + HALO) * CHUNKS + c
        down_ref[at : at + 1, :] = cy_ref[0, 0:1, LANES * c : LANES * (c + 1)]
    up_ref[UP_ROWS - 5 :, :] = jnp.zeros((5, LANES), F32)
    down_ref[DOWN_ROWS - 4 :, :] = jnp.zeros((4, LANES), F32)


def split_bf16(x):
    high = x.astype(BF16)
    return high, (x - high.astype(F32)).astype(BF16)


def dot_parts(x, basis_high, basis_low, dims):
    high, low = split_bf16(x)
    rows = x.shape[0]
    both = lax.dot_general(
        jnp.concatenate([high, low], axis=0), basis_high, dims, preferred_element_type=F32
    )
    small = lax.dot_general(high, basis_low, dims, preferred_element_type=F32)
    return both[:rows] + both[rows:] + small


FORWARD = (((1,), (0,)), ((), ()))
BACKWARD = (((1,), (1,)), ((), ()))


def filter_tables():
    b = np.arange(LANES)
    m = np.arange(LANES)
    blocks = []
    for s in range(1, 5):
        angle = 2.0 * np.pi * ((b[:, None] * (CHUNKS * m[None] + s)) % NLON) / NLON
        cos, sin = np.cos(angle), np.sin(angle)
        blocks.append(np.block([[cos, -sin], [sin, cos]]))
    angle = 2.0 * np.pi * ((b[:, None] * m[None]) % LANES) / LANES
    zero = np.where(m[None] <= LANES // 2, np.cos(angle), np.sin(angle))
    wide = np.stack(blocks)

    def halves(x):
        high = x.astype(np.float32).astype(ml_dtypes.bfloat16)
        low = (x - high.astype(np.float64)).astype(np.float32).astype(ml_dtypes.bfloat16)
        return np.stack([high, low])

    waves = np.concatenate([CHUNKS * m + s for s in range(5)])
    sines = np.sin(np.pi * waves / NLON)
    limit = np.where(waves == 0, 1e30, 4.0 / np.where(waves == 0, 1.0, sines * sines))
    weight = np.full(waves.shape, 2.0 / NLON)
    weight[0] = 1.0 / NLON
    weight[LANES // 2] = 1.0 / NLON
    table = np.zeros((8, waves.size), np.float32)
    table[0], table[1] = limit, weight
    return halves(wide), halves(zero), table


def smooth(band, z_scr, spec_scr, wide_ref, zero_ref, table_ref):
    first = (band * ROWS).astype(F32)
    ids = first + lax.broadcasted_iota(jnp.int32, (16, LANES), 0).astype(F32)
    centre = jnp.sin(math.pi * (ids + 0.5) / NLAT)[:, :1]
    damping = jnp.minimum(1.0, centre * centre * table_ref[0:1, :]) * table_ref[1:2, :]
    cells = ROWS * NT
    x = [z_scr[:, LANES * a : LANES * (a + 1)] for a in range(CHUNKS)]
    plus = [x[a] + x[CHUNKS - a] for a in range(1, 5)]
    minus = [x[a] - x[CHUNKS - a] for a in range(1, 5)]

    def damp(block):
        rows = [
            jnp.broadcast_to(damping[r : r + 1, LANES * block : LANES * (block + 1)], (NT, LANES))
            for r in range(ROWS)
        ]
        return jnp.concatenate(rows, axis=0)

    total = x[0] + plus[0] + plus[1] + plus[2] + plus[3]
    spectrum = dot_parts(total, zero_ref[0], zero_ref[1], FORWARD) * damp(0)
    spec_scr[:, 0:LANES] = dot_parts(spectrum, zero_ref[0], zero_ref[1], BACKWARD)
    for s in range(1, 5):
        real, imag = x[0], None
        for a in range(1, 5):
            angle = 2.0 * math.pi * (s * a % CHUNKS) / CHUNKS
            real = real + plus[a - 1] * math.cos(angle)
            term = minus[a - 1] * -math.sin(angle)
            imag = term if imag is None else imag + term
        spectrum = dot_parts(
            jnp.concatenate([real, imag], axis=1), wide_ref[0, s - 1], wide_ref[1, s - 1], FORWARD
        )
        factor = damp(s)
        spectrum = spectrum * jnp.concatenate([factor, factor], axis=1)
        at = LANES * (2 * s - 1)
        spec_scr[:, at : at + 2 * LANES] = dot_parts(
            spectrum, wide_ref[0, s - 1], wide_ref[1, s - 1], BACKWARD
        )
    mean = spec_scr[:, 0:LANES]
    real = [spec_scr[:, LANES * (2 * s - 1) : LANES * 2 * s] for s in range(1, 5)]
    imag = [spec_scr[:, LANES * 2 * s : LANES * (2 * s + 1)] for s in range(1, 5)]
    z_scr[:, 0:LANES] = mean + real[0] + real[1] + real[2] + real[3]
    for a in range(1, 5):
        even, odd = mean, None
        for s in range(1, 5):
            angle = 2.0 * math.pi * (s * a % CHUNKS) / CHUNKS
            even = even + real[s - 1] * math.cos(angle)
            term = imag[s - 1] * math.sin(angle)
            odd = term if odd is None else odd + term
        z_scr[:, LANES * a : LANES * (a + 1)] = even - odd
        b = CHUNKS - a
        z_scr[:, LANES * b : LANES * (b + 1)] = even + odd


def combine(r, weights, q_of, z_row):
    total = row_of(weights, 7, r) * z_row
    for d in range(7):
        total = total + row_of(weights, d, r) * q_of(r + d - HALO)
    return total


def inner_kernel(
    q_in, h_in, cx_in, cy_in, wide_ref, zero_ref, table_ref,
    msg, q_out, z_out, base_out,
    cx_scr, hx_scr, cy_scr, e_scr, wx_scr, wy_scr, z_scr, spec_scr,
):
    band = lax.axis_index("lat")
    blank = jnp.zeros((4, NLON), F32)
    hx_scr[...] = jnp.zeros(hx_scr.shape, F32)
    hx_scr[HALO : HALO + ROWS] = h_in[0]
    cx_scr[0:ROWS] = cx_in[0]
    cx_scr[ROWS:16] = blank
    cy_scr[0:ROWS] = cy_in[0]
    cy_scr[ROWS:16] = blank
    h = hx_scr[HALO : HALO + 16]
    c = cx_scr[...]
    n, k, w, positive = face_coefs(c)
    west = shifted(h, -1)
    edge = (7.0 / 12.0) * (west + h) - (1.0 / 12.0) * (shifted(h, -2) + shifted(h, 1))
    far = jnp.where(positive, shifted(edge, -1), shifted(edge, 1))
    mass = c * (n * edge + k * jnp.where(positive, west, h) + w * far)
    base = h - (shifted(mass, 1) - mass)
    faces = flux_stencil(mass, n, k, w, positive)
    stencil = divergence_stencil(faces, lambda f: shifted(f, 1))
    for d in range(7):
        wx_scr[d] = stencil[d]
    base_out[...] = base
    for r in range(ROWS):
        row = q_in[:, 0, r, :]
        q_out[r] = row
        total = row_of(wx_scr, 3, r) * row
        for d in (-3, -2, -1, 1, 2, 3):
            total = total + row_of(wx_scr, d + 3, r) * shifted(row, d)
        z_scr[NT * r : NT * (r + 1), :] = total

    south, north = band * ROWS, NLAT - 1 - (band * ROWS + ROWS - 1)

    @pl.when(jnp.minimum(south, north) < NLAT // 6)
    def _():
        smooth(band, z_scr, spec_scr, wide_ref, zero_ref, table_ref)

    new_thick = meridional(band, hx_scr, cy_scr, e_scr, base, wy_scr)

    def ratio_row(r):
        return combine(r, wy_scr, lambda j: q_out[j], z_scr[NT * r : NT * (r + 1), :])

    pack_message(INNER, ratio_row, new_thick, msg)
    for v, r in enumerate(OUTER):
        z_out[v] = z_scr[NT * r : NT * (r + 1), :]


def outer_kernel(
    q_ref, z_ref, base_ref, h_in, cy_in, south_ref, north_ref,
    msg,
    hx_scr, cy_scr, e_scr, wy_scr,
):
    band = lax.axis_index("lat")
    hx_scr[HALO : HALO + ROWS] = h_in[0]
    hx_scr[ROWS + 2 * HALO : 24] = jnp.zeros((24 - ROWS - 2 * HALO, NLON), F32)
    cy_scr[0:ROWS] = cy_in[0]
    cy_scr[ROWS:16] = jnp.zeros((4, NLON), F32)
    for c in range(CHUNKS):
        at = 8 * CHUNKS * HALO + HALO * c
        lanes = slice(LANES * c, LANES * (c + 1))
        hx_scr[0:HALO, lanes] = south_ref[at : at + HALO, :]
        hx_scr[HALO + ROWS : ROWS + 2 * HALO, lanes] = north_ref[at : at + HALO, :]
        at = (8 * HALO + HALO) * CHUNKS + c
        cy_scr[ROWS : ROWS + 1, lanes] = north_ref[at : at + 1, :]
    new_thick = meridional(band, hx_scr, cy_scr, e_scr, base_ref[...], wy_scr)

    def tile_row(ref, i):
        at = 8 * CHUNKS * i
        return jnp.concatenate(
            [ref[at + 8 * c : at + 8 * c + 8, :] for c in range(CHUNKS)], axis=1
        )

    def q_of(j):
        if j < 0:
            return tile_row(south_ref, j + HALO)
        if j >= ROWS:
            return tile_row(north_ref, j - ROWS)
        return q_ref[j]

    def ratio_row(r):
        return combine(r, wy_scr, q_of, z_ref[OUTER.index(r)])

    pack_message(OUTER, ratio_row, new_thick, msg)


def remap_kernel(weight_ref, first_ref, second_ref, out_ref, mass_ref, inter_scr, main_scr, tail_scr):
    weight_sum = weight_ref[0]
    for k in range(1, NLEV):
        weight_sum = weight_sum + weight_ref[k]
    lanes = lane_ids()
    base = 8 * HALF + 8
    for in_ref, rows in ((first_ref, INNER), (second_ref, OUTER)):
        thick = [in_ref[i, base : base + 8, :] for i in range(NLEV)]
        upper, lower = [thick[0]], []
        for i in range(1, NLEV):
            upper.append(upper[-1] + thick[i])
        for i in range(NLEV):
            lower.append(upper[i] - thick[i])
        total = upper[-1]
        for v, r in enumerate(rows):
            mass_ref[r : r + 1, 0:LANES] = total[v : v + 1]
            mass_ref[r : r + 1, LANES:PIECE] = turn(total[HALF : HALF + 1], -TAIL * v)[:, :TAIL]
        reach = None
        for k in range(NLEV):
            target = total * (weight_ref[k] / weight_sum)
            reach = target if reach is None else reach + target
            start = reach - target
            scale = 1.0 / target
            for i in range(NLEV):
                overlap = jnp.minimum(upper[i], reach) - jnp.maximum(lower[i], start)
                inter_scr[NLEV * k + i] = jnp.maximum(overlap, 0.0) * scale
        for v in range(HALF + 1):
            ratio = [in_ref[i, 8 * v : 8 * v + 8, :] for i in range(NLEV)]
            for k in range(NLEV):
                moved = None
                for i in range(NLEV):
                    share = jnp.broadcast_to(inter_scr[NLEV * k + i, v : v + 1, :], (NT, LANES))
                    term = ratio[i] * share
                    moved = term if moved is None else moved + term
                if v < HALF:
                    main_scr[k, rows[v]] = moved
                else:
                    for u, r in enumerate(rows):
                        tail_scr[k, r] = turn(moved, -TAIL * u)
    for k in range(NLEV):
        main = jnp.swapaxes(main_scr[k], 0, 1)
        tail = jnp.swapaxes(tail_scr[k], 0, 1)
        out_ref[:, k, :, 0:LANES] = main[:, 0:ROWS, :]
        out_ref[:, k, :, LANES:PIECE] = tail[:, 0:ROWS, 0:TAIL]


def shape(*dims):
    return jax.ShapeDtypeStruct(dims, F32)


def scratch(*dims):
    return pltpu.VMEM(dims, F32)


def local(tracers, thickness, courant_x, courant_y, level_weights):
    bands = lax.axis_size("lat")
    wide, zero, table = filter_tables()
    up, down = pl.pallas_call(
        edge_kernel,
        out_shape=(shape(UP_ROWS, LANES), shape(DOWN_ROWS, LANES)),
        in_specs=[vmem()] * 3,
        out_specs=(vmem(),) * 2,
        compiler_params=params(16),
        name="edge_rows",
    )(tracers, thickness, courant_y)
    south = lax.ppermute(up, "lat", [(i, i + 1) for i in range(bands - 1)])
    north = lax.ppermute(down, "lat", [(i + 1, i) for i in range(bands - 1)])
    first, q, z, base = pl.pallas_call(
        inner_kernel,
        out_shape=(
            shape(NLEV, MSG, LANES), shape(ROWS, NT, NLON), shape(HALF, NT, NLON), shape(16, NLON),
        ),
        in_specs=[vmem()] * 7,
        out_specs=(vmem(),) * 4,
        scratch_shapes=[
            scratch(16, NLON), scratch(24, NLON), scratch(16, NLON), scratch(24, NLON),
            scratch(7, 16, NLON), scratch(8, 16, NLON),
            scratch(ROWS * NT, NLON), scratch(ROWS * NT, NLON),
        ],
        compiler_params=params(32),
        name="inner_rows",
    )(tracers, thickness, courant_x, courant_y, jnp.asarray(wide), jnp.asarray(zero), jnp.asarray(table))
    first = lax.all_to_all(first, "lev", split_axis=0, concat_axis=0, tiled=True)
    second = pl.pallas_call(
        outer_kernel,
        out_shape=shape(NLEV, MSG, LANES),
        in_specs=[vmem()] * 7,
        out_specs=vmem(),
        scratch_shapes=[
            scratch(24, NLON), scratch(16, NLON), scratch(24, NLON), scratch(8, 16, NLON),
        ],
        compiler_params=params(32),
        name="outer_rows",
    )(q, z, base, thickness, courant_y, south, north)
    second = lax.all_to_all(second, "lev", split_axis=0, concat_axis=0, tiled=True)
    remapped, column_mass = pl.pallas_call(
        remap_kernel,
        out_shape=(shape(NT, NLEV, ROWS, PIECE), shape(ROWS, PIECE)),
        in_specs=[pl.BlockSpec(memory_space=pltpu.SMEM), vmem(), vmem()],
        out_specs=(vmem(),) * 2,
        scratch_shapes=[scratch(NLEV * NLEV, 8, LANES), scratch(NLEV, 16, NT, LANES), scratch(NLEV, 16, NT, LANES)],
        compiler_params=params(32),
        name="remap",
    )(level_weights, first, second)
    return remapped, column_mass


def solution(mesh):
    placed = (
        P(None, "lev", "lat", None),
        P("lev", "lat", None),
        P("lev", "lat", None),
        P("lev", "lat", None),
        P(),
    )
    return jax.shard_map(
        local,
        mesh=mesh,
        in_specs=placed,
        out_specs=(P(None, None, "lat", "lev"), P("lat", "lev")),
        check_vma=False,
    )
```

```python
import math

import jax
import jax.numpy as jnp
import ml_dtypes
import numpy as np
from jax import lax
from jax.experimental import pallas as pl
from jax.experimental.pallas import tpu as pltpu
from jax.sharding import PartitionSpec as P

NT = 8
NLEV = 8
NLAT = 768
NLON = 1152
ROWS = 12
LANES = 128
CHUNKS = NLON // LANES
PIECE = NLON // NLEV
TAIL = PIECE - LANES
HALO = 3
INNER = tuple(range(HALO, ROWS - HALO))
OUTER = tuple(range(HALO)) + tuple(range(ROWS - HALO, ROWS))
HALF = ROWS // 2
MSG = 64
SEND = 256
ZFLOPS = 2 * 10**10
ZBYTES = 10**10
WHOLE = 62
F32 = jnp.float32
BF16 = jnp.bfloat16


def vmem():
    return pl.BlockSpec(memory_space=pltpu.VMEM)


def far():
    return pl.BlockSpec(memory_space=pltpu.HBM)


def copies(semaphores, *pairs):
    return [
        pltpu.make_async_copy(source, target, semaphores.at[i])
        for i, (source, target) in enumerate(pairs)
    ]


def params(mib):
    return pltpu.CompilerParams(vmem_limit_bytes=mib * 1024 * 1024)


def shifted(x, d):
    return x if d == 0 else pltpu.roll(x, (-d) % NLON, 1)


def face_coefs(courant):
    m = jnp.abs(courant)
    k = m * (3.0 - 2.0 * m)
    return 1.0 - 0.5 * (m + k), k, 0.5 * (m - k), courant > 0.0


def flux_stencil(mass, n, k, w, positive):
    zero = jnp.zeros_like(mass)
    a, b, c = mass * n, mass * k, mass * w
    bp, cp = jnp.where(positive, b, zero), jnp.where(positive, c, zero)
    bm, cm = b - bp, c - cp
    s, t = 7.0 / 12.0, 1.0 / 12.0
    return (
        -t * cp,
        s * cp - t * a,
        s * (a + cp) - t * cm + bp,
        s * (a + cm) - t * cp + bm,
        s * cm - t * a,
        -t * cm,
    )


def divergence_stencil(faces, ahead):
    nxt = [ahead(f) for f in faces]
    return (
        [-faces[0]] + [nxt[i] - faces[i + 1] for i in range(5)] + [nxt[5]]
    )


def meridional(band, hx, cy, e_scr, base, store):
    first = (band * ROWS).astype(F32)
    ids = first + lax.broadcasted_iota(jnp.int32, (16, LANES), 0).astype(F32)
    centre = jnp.sin(math.pi * (ids + 0.5) / NLAT)[:, :1]
    face_cos = jnp.sin(math.pi * ids / NLAT)[:, :1]
    e_scr[0:16] = (7.0 / 12.0) * (hx[1:17] + hx[2:18]) - (1.0 / 12.0) * (hx[0:16] + hx[3:19])
    e_scr[16:24] = jnp.zeros((8, NLON), F32)
    c = cy[...]
    n, k, w, positive = face_coefs(c)
    cell = jnp.where(positive, hx[2:18], hx[3:19])
    far = jnp.where(positive, e_scr[0:16], e_scr[2:18])
    mass = c * face_cos * (n * e_scr[1:17] + k * cell + w * far)
    faces = flux_stencil(mass, n, k, w, positive)

    def ahead(x):
        return pltpu.roll(x, 15, 0)

    stencil = divergence_stencil(faces, ahead)
    per_centre = 1.0 / centre
    new_thick = base - (ahead(mass) - mass) * per_centre
    inverse = 1.0 / new_thick
    scale = inverse * per_centre
    for d in range(7):
        weight = -stencil[d] * scale
        if d == 3:
            weight = weight + hx[3:19] * inverse
        store[d] = weight
    store[7] = -inverse
    return new_thick


def row_of(ref, index, row):
    return jnp.broadcast_to(ref[index, row : row + 1, :], (NT, NLON))


def lane_ids(rows=NT):
    return lax.broadcasted_iota(jnp.int32, (rows, LANES), 1)


def turn(x, amount):
    amount %= LANES
    return x if amount == 0 else pltpu.roll(x, amount, 1)


def window(lanes, low, high, dest):
    if dest == 0:
        return low
    keep = lanes < LANES - TAIL * dest
    return jnp.where(keep, turn(low, -TAIL * dest), turn(high, -TAIL * dest))


def pack_message(rows, ratio_row, new_thick, msg):
    lanes = lane_ids()
    tails = [jnp.zeros((NT, LANES), F32)] * NLEV
    for v, r in enumerate(rows):
        ratio = ratio_row(r)
        part = [ratio[:, LANES * c : LANES * (c + 1)] for c in range(CHUNKS)]
        here = (lanes >= TAIL * v) & (lanes < TAIL * (v + 1))
        for dest in range(NLEV):
            msg[dest, 8 * v : 8 * v + 8, :] = window(lanes, part[dest], part[dest + 1], dest)
            tails[dest] = jnp.where(here, turn(part[dest + 1], TAIL * (v - dest)), tails[dest])
    for dest in range(NLEV):
        msg[dest, 8 * HALF : 8 * HALF + 8, :] = tails[dest]
    lanes16 = lane_ids(16)
    wide = lane_ids(1)
    base = 8 * HALF + 8
    for dest in range(NLEV):
        low = new_thick[:, LANES * dest : LANES * (dest + 1)]
        high = new_thick[:, LANES * (dest + 1) : LANES * (dest + 2)]
        main = window(lanes16, low, high, dest)
        last = jnp.ones((1, LANES), F32)
        for v, r in enumerate(rows):
            msg[dest, base + v : base + v + 1, :] = main[r : r + 1]
            here = (wide >= TAIL * v) & (wide < TAIL * (v + 1))
            last = jnp.where(here, turn(high[r : r + 1], TAIL * (v - dest)), last)
        msg[dest, base + HALF : base + HALF + 1, :] = last
        msg[dest, base + HALF + 1 : base + HALF + 2, :] = jnp.ones((1, LANES), F32)


def tracer_tile(ref, row, chunk):
    return ref[pl.ds(CHUNKS * row + chunk, NT, stride=CHUNKS * ROWS), :]


def edge_kernel(
    q_in, h_in, cy_in,
    odd_ref, even_ref,
    q_ref, h_ref, cy_ref, semaphores,
):
    band = lax.axis_index("lat")
    loads = copies(semaphores, (q_in, q_ref), (h_in, h_ref), (cy_in, cy_ref))
    for load in loads:
        load.start()
    for load in loads:
        load.wait()

    def put(ref, first):
        for i in range(HALO):
            for c in range(CHUNKS):
                at = 8 * (CHUNKS * i + c)
                ref[at : at + 8, :] = tracer_tile(q_ref, first + i, c)
        at = 8 * CHUNKS * HALO
        size = CHUNKS * HALO
        for i in range(size):
            ref[at + i : at + i + 1, :] = h_ref[CHUNKS * first + i]
        for i in range(CHUNKS):
            ref[at + size + i : at + size + i + 1, :] = cy_ref[i]
        ref[at + size + CHUNKS : SEND, :] = jnp.zeros((SEND - at - size - CHUNKS, LANES), F32)

    @pl.when(band % 2 == 0)
    def _():
        put(even_ref, ROWS - HALO)
        put(odd_ref, 0)

    @pl.when(band % 2 == 1)
    def _():
        put(odd_ref, ROWS - HALO)
        put(even_ref, 0)


def split_bf16(x):
    high = x.astype(BF16)
    return high, (x - high.astype(F32)).astype(BF16)


def dot_parts(x, basis_high, basis_low, dims):
    high, low = split_bf16(x)
    rows = x.shape[0]
    both = lax.dot_general(
        jnp.concatenate([high, low], axis=0), basis_high, dims, preferred_element_type=F32
    )
    small = lax.dot_general(high, basis_low, dims, preferred_element_type=F32)
    return both[:rows] + both[rows:] + small


FORWARD = (((1,), (0,)), ((), ()))
BACKWARD = (((1,), (1,)), ((), ()))


def filter_tables():
    b = np.arange(LANES)
    m = np.arange(LANES)
    blocks = []
    for s in range(1, 5):
        angle = 2.0 * np.pi * ((b[:, None] * (CHUNKS * m[None] + s)) % NLON) / NLON
        cos, sin = np.cos(angle), np.sin(angle)
        blocks.append(np.block([[cos, -sin], [sin, cos]]))
    angle = 2.0 * np.pi * ((b[:, None] * m[None]) % LANES) / LANES
    zero = np.where(m[None] <= LANES // 2, np.cos(angle), np.sin(angle))
    wide = np.stack(blocks)

    def halves(x):
        high = x.astype(np.float32).astype(ml_dtypes.bfloat16)
        low = (x - high.astype(np.float64)).astype(np.float32).astype(ml_dtypes.bfloat16)
        return np.stack([high, low])

    waves = np.concatenate([CHUNKS * m + s for s in range(5)])
    sines = np.sin(np.pi * waves / NLON)
    limit = np.where(waves == 0, 1e30, 4.0 / np.where(waves == 0, 1.0, sines * sines))
    weight = np.full(waves.shape, 2.0 / NLON)
    weight[0] = 1.0 / NLON
    weight[LANES // 2] = 1.0 / NLON
    table = np.zeros((8, waves.size), np.float32)
    table[0], table[1] = limit, weight
    return halves(wide), halves(zero), table


def smooth(band, rows, z_scr, spec_scr, wide_ref, zero_ref, table_ref):
    first = (band * ROWS).astype(F32)
    ids = first + lax.broadcasted_iota(jnp.int32, (16, LANES), 0).astype(F32)
    centre = jnp.sin(math.pi * (ids + 0.5) / NLAT)[:, :1]
    damping = jnp.minimum(1.0, centre * centre * table_ref[0:1, :]) * table_ref[1:2, :]
    x = [z_scr[:, LANES * a : LANES * (a + 1)] for a in range(CHUNKS)]
    plus = [x[a] + x[CHUNKS - a] for a in range(1, 5)]
    minus = [x[a] - x[CHUNKS - a] for a in range(1, 5)]

    def damp(block):
        blocks = [
            jnp.broadcast_to(damping[r : r + 1, LANES * block : LANES * (block + 1)], (NT, LANES))
            for r in rows
        ]
        return jnp.concatenate(blocks, axis=0)

    total = x[0] + plus[0] + plus[1] + plus[2] + plus[3]
    spectrum = dot_parts(total, zero_ref[0], zero_ref[1], FORWARD) * damp(0)
    spec_scr[:, 0:LANES] = dot_parts(spectrum, zero_ref[0], zero_ref[1], BACKWARD)
    for s in range(1, 5):
        real, imag = x[0], None
        for a in range(1, 5):
            angle = 2.0 * math.pi * (s * a % CHUNKS) / CHUNKS
            real = real + plus[a - 1] * math.cos(angle)
            term = minus[a - 1] * -math.sin(angle)
            imag = term if imag is None else imag + term
        spectrum = dot_parts(
            jnp.concatenate([real, imag], axis=1), wide_ref[0, s - 1], wide_ref[1, s - 1], FORWARD
        )
        factor = damp(s)
        spectrum = spectrum * jnp.concatenate([factor, factor], axis=1)
        at = LANES * (2 * s - 1)
        spec_scr[:, at : at + 2 * LANES] = dot_parts(
            spectrum, wide_ref[0, s - 1], wide_ref[1, s - 1], BACKWARD
        )
    mean = spec_scr[:, 0:LANES]
    real = [spec_scr[:, LANES * (2 * s - 1) : LANES * 2 * s] for s in range(1, 5)]
    imag = [spec_scr[:, LANES * 2 * s : LANES * (2 * s + 1)] for s in range(1, 5)]
    z_scr[:, 0:LANES] = mean + real[0] + real[1] + real[2] + real[3]
    for a in range(1, 5):
        even, odd = mean, None
        for s in range(1, 5):
            angle = 2.0 * math.pi * (s * a % CHUNKS) / CHUNKS
            even = even + real[s - 1] * math.cos(angle)
            term = imag[s - 1] * math.sin(angle)
            odd = term if odd is None else odd + term
        z_scr[:, LANES * a : LANES * (a + 1)] = even - odd
        b = CHUNKS - a
        z_scr[:, LANES * b : LANES * (b + 1)] = even + odd


def combine(r, weights, q_of, z_row):
    total = row_of(weights, 7, r) * z_row
    for d in range(7):
        total = total + row_of(weights, d, r) * q_of(r + d - HALO)
    return total


def spread(ref, scr, at):
    for r in range(ROWS):
        for c in range(CHUNKS):
            scr[at + r : at + r + 1, LANES * c : LANES * (c + 1)] = ref[CHUNKS * r + c]


def is_polar(band):
    south, north = band * ROWS, NLAT - 1 - (band * ROWS + ROWS - 1)
    return jnp.minimum(south, north) < NLAT // 6


def zonal(rows, q_in, h_in, cx_in, cx_scr, hx_scr, wx_scr, z_scr, smooth_rows):
    band = lax.axis_index("lat")
    hx_scr[...] = jnp.zeros(hx_scr.shape, F32)
    spread(h_in, hx_scr, HALO)
    spread(cx_in, cx_scr, 0)
    cx_scr[ROWS:16] = jnp.zeros((4, NLON), F32)
    h = hx_scr[HALO : HALO + 16]
    c = cx_scr[...]
    n, k, w, positive = face_coefs(c)
    west = shifted(h, -1)
    edge = (7.0 / 12.0) * (west + h) - (1.0 / 12.0) * (shifted(h, -2) + shifted(h, 1))
    far = jnp.where(positive, shifted(edge, -1), shifted(edge, 1))
    mass = c * (n * edge + k * jnp.where(positive, west, h) + w * far)
    faces = flux_stencil(mass, n, k, w, positive)
    stencil = divergence_stencil(faces, lambda f: shifted(f, 1))
    for d in range(7):
        wx_scr[d] = stencil[d]
    for v, r in enumerate(rows):
        row = tracer_row(q_in, r)
        total = row_of(wx_scr, 3, r) * row
        for d in (-3, -2, -1, 1, 2, 3):
            total = total + row_of(wx_scr, d + 3, r) * shifted(row, d)
        z_scr[NT * v : NT * (v + 1), :] = total

    @pl.when(is_polar(band))
    def _():
        smooth_rows(band)

    return h - (shifted(mass, 1) - mass)


def tracer_row(ref, row):
    return jnp.concatenate([tracer_tile(ref, row, chunk) for chunk in range(CHUNKS)], axis=1)


def inner_kernel(
    q_far, h_far, cx_far, cy_far, wide_far, zero_far, table_far, _sent,
    msg,
    cx_scr, hx_scr, cy_scr, e_scr, wx_scr, wy_scr, z_scr, spec_scr, q_scr,
    q_in, h_in, cx_in, cy_in, wide_ref, zero_ref, table_ref, semaphores,
):
    band = lax.axis_index("lat")
    *fields, wide_load, zero_load, table_load = copies(
        semaphores, (q_far, q_in), (h_far, h_in), (cx_far, cx_in), (cy_far, cy_in),
        (wide_far, wide_ref), (zero_far, zero_ref), (table_far, table_ref),
    )
    loads = (wide_load, zero_load, table_load)
    for load in fields:
        load.start()

    @pl.when(is_polar(band))
    def _():
        for load in loads:
            load.start()

    def smooth_rows(band):
        for load in loads:
            load.wait()
        smooth(band, INNER, z_scr, spec_scr, wide_ref, zero_ref, table_ref)

    for load in fields:
        load.wait()
    base = zonal(INNER, q_in, h_in, cx_in, cx_scr, hx_scr, wx_scr, z_scr, smooth_rows)
    spread(cy_in, cy_scr, 0)
    cy_scr[ROWS:16] = jnp.zeros((4, NLON), F32)
    new_thick = meridional(band, hx_scr, cy_scr, e_scr, base, wy_scr)
    for r in range(ROWS):
        q_scr[r] = tracer_row(q_in, r)

    def ratio_row(r):
        v = INNER.index(r)
        return combine(r, wy_scr, lambda j: q_scr[j], z_scr[NT * v : NT * (v + 1), :])

    pack_message(INNER, ratio_row, new_thick, msg)


def zonal_kernel(
    q_in, h_in, cx_in, wide_ref, zero_ref, table_ref,
    z_out, base_out,
    cx_scr, hx_scr, wx_scr, spec_scr,
):
    def smooth_rows(band):
        smooth(band, OUTER, z_out, spec_scr, wide_ref, zero_ref, table_ref)

    base_out[...] = zonal(OUTER, q_in, h_in, cx_in, cx_scr, hx_scr, wx_scr, z_out, smooth_rows)


def outer_kernel(
    q_in, z_ref, base_ref, h_in, cy_in, odd_ref, even_ref,
    msg,
    hx_scr, cy_scr, e_scr, wy_scr, q_scr,
):
    band = lax.axis_index("lat")
    spread(h_in, hx_scr, HALO)
    hx_scr[ROWS + 2 * HALO : 24] = jnp.zeros((24 - ROWS - 2 * HALO, NLON), F32)
    spread(cy_in, cy_scr, 0)
    cy_scr[ROWS:16] = jnp.zeros((4, NLON), F32)

    def take(south_ref, north_ref):
        for i in range(HALO):
            for c in range(CHUNKS):
                at = 8 * (CHUNKS * i + c)
                lanes = slice(LANES * c, LANES * (c + 1))
                q_scr[i, :, lanes] = south_ref[at : at + 8, :]
                q_scr[HALO + ROWS + i, :, lanes] = north_ref[at : at + 8, :]
        for c in range(CHUNKS):
            at = 8 * CHUNKS * HALO + c
            lanes = slice(LANES * c, LANES * (c + 1))
            hx_scr[0:HALO, lanes] = south_ref[pl.ds(at, HALO, stride=CHUNKS), :]
            hx_scr[HALO + ROWS : ROWS + 2 * HALO, lanes] = north_ref[pl.ds(at, HALO, stride=CHUNKS), :]
            at = at + CHUNKS * HALO
            cy_scr[ROWS : ROWS + 1, lanes] = north_ref[at : at + 1, :]

    @pl.when(band % 2 == 0)
    def _():
        take(odd_ref, even_ref)

    @pl.when(band % 2 == 1)
    def _():
        take(even_ref, odd_ref)

    new_thick = meridional(band, hx_scr, cy_scr, e_scr, base_ref[...], wy_scr)

    for r in range(ROWS):
        q_scr[HALO + r] = tracer_row(q_in, r)

    def ratio_row(r):
        v = OUTER.index(r)
        return combine(r, wy_scr, lambda j: q_scr[HALO + j], z_ref[NT * v : NT * (v + 1), :])

    pack_message(OUTER, ratio_row, new_thick, msg)


def remap_kernel(weight_ref, first_ref, second_ref, out_ref, mass_ref, inter_scr):
    weight_sum = weight_ref[0]
    for k in range(1, NLEV):
        weight_sum = weight_sum + weight_ref[k]
    base = 8 * HALF + 8
    for in_ref, rows in ((first_ref, INNER), (second_ref, OUTER)):
        thick = [in_ref[i, base : base + 8, :] for i in range(NLEV)]
        upper, lower = [thick[0]], []
        for i in range(1, NLEV):
            upper.append(upper[-1] + thick[i])
        for i in range(NLEV):
            lower.append(upper[i] - thick[i])
        total = upper[-1]
        for v, r in enumerate(rows):
            mass_ref[r : r + 1, 0:LANES] = total[v : v + 1]
            mass_ref[r : r + 1, LANES:PIECE] = turn(total[HALF : HALF + 1], -TAIL * v)[:, :TAIL]
        reach = None
        for k in range(NLEV):
            target = total * (weight_ref[k] / weight_sum)
            reach = target if reach is None else reach + target
            start = reach - target
            scale = 1.0 / target
            for i in range(NLEV):
                overlap = jnp.minimum(upper[i], reach) - jnp.maximum(lower[i], start)
                at = 8 * (NLEV * i + k)
                inter_scr[at : at + 8, :] = jnp.maximum(overlap, 0.0) * scale
        for v in range(HALF + 1):
            moved = [None] * NT
            for i in range(NLEV):
                share = inter_scr[pl.ds(8 * NLEV * i + v, NLEV, stride=8), :]
                for t in range(NT):
                    at = 8 * v + t
                    term = jnp.broadcast_to(in_ref[i, at : at + 1, :], (NLEV, LANES)) * share
                    moved[t] = term if i == 0 else moved[t] + term
            for t in range(NT):
                if v < HALF:
                    out_ref[t, rows[v], :, 0:LANES] = moved[t]
                else:
                    for u, r in enumerate(rows):
                        out_ref[t, r, :, LANES:PIECE] = turn(moved[t], -TAIL * u)[:, :TAIL]


def swaps(first, bands):
    low = range(first, bands - 1, 2)
    return [(i, i + 1) for i in low] + [(i + 1, i) for i in low]


def shape(*dims):
    return jax.ShapeDtypeStruct(dims, F32)


def scratch(*dims):
    return pltpu.VMEM(dims, F32)


def local(tracers, thickness, courant_x, courant_y, level_weights):
    bands = lax.axis_size("lat")
    wide, zero, table = filter_tables()
    q_in = tracers.reshape(NT * ROWS * CHUNKS, LANES)
    h_in, cx_in, cy_in = (
        field.reshape(ROWS * CHUNKS, 1, LANES) for field in (thickness, courant_x, courant_y)
    )
    odd, even = pl.pallas_call(
        edge_kernel,
        out_shape=(shape(SEND, LANES),) * 2,
        in_specs=[far()] * 3,
        out_specs=(vmem(),) * 2,
        scratch_shapes=[
            scratch(NT * ROWS * CHUNKS, LANES), scratch(ROWS * CHUNKS, 1, LANES),
            scratch(ROWS * CHUNKS, 1, LANES), pltpu.SemaphoreType.DMA((3,)),
        ],
        compiler_params=params(WHOLE),
        name="edge_rows",
    )(q_in, h_in, cy_in)
    sent = odd
    odd = lax.ppermute(odd, "lat", swaps(1, bands))
    even = lax.ppermute(even, "lat", swaps(0, bands))
    tables = (jnp.asarray(wide), jnp.asarray(zero), jnp.asarray(table))
    first = pl.pallas_call(
        inner_kernel,
        out_shape=shape(NLEV, MSG, LANES),
        in_specs=[far()] * 8,
        out_specs=vmem(),
        scratch_shapes=[
            scratch(16, NLON), scratch(24, NLON), scratch(16, NLON), scratch(24, NLON),
            scratch(7, 16, NLON), scratch(8, 16, NLON),
            scratch(HALF * NT, NLON), scratch(HALF * NT, NLON), scratch(ROWS, NT, NLON),
            scratch(NT * ROWS * CHUNKS, LANES),
        ]
        + [scratch(ROWS * CHUNKS, 1, LANES)] * 3
        + [pltpu.VMEM(t.shape, t.dtype) for t in tables]
        + [pltpu.SemaphoreType.DMA((7,))],
        compiler_params=params(WHOLE),
        name="inner_rows",
    )(q_in, h_in, cx_in, cy_in, *tables, sent)
    first = lax.all_to_all(first, "lev", split_axis=0, concat_axis=0, tiled=True)
    z, base = pl.pallas_call(
        zonal_kernel,
        out_shape=(shape(HALF * NT, NLON), shape(16, NLON)),
        in_specs=[vmem()] * 6,
        out_specs=(vmem(),) * 2,
        scratch_shapes=[
            scratch(16, NLON), scratch(24, NLON), scratch(7, 16, NLON), scratch(HALF * NT, NLON),
        ],
        compiler_params=params(32),
        cost_estimate=pl.CostEstimate(flops=ZFLOPS, bytes_accessed=ZBYTES, transcendentals=0),
        name="outer_zonal",
    )(q_in, h_in, cx_in, *tables)
    second = pl.pallas_call(
        outer_kernel,
        out_shape=shape(NLEV, MSG, LANES),
        in_specs=[vmem()] * 7,
        out_specs=vmem(),
        scratch_shapes=[
            scratch(24, NLON), scratch(16, NLON), scratch(24, NLON), scratch(8, 16, NLON),
            scratch(ROWS + 2 * HALO, NT, NLON),
        ],
        compiler_params=params(32),
        name="outer_rows",
    )(q_in, z, base, h_in, cy_in, odd, even)
    second = lax.all_to_all(second, "lev", split_axis=0, concat_axis=0, tiled=True)
    remapped, column_mass = pl.pallas_call(
        remap_kernel,
        out_shape=(shape(NT, ROWS, NLEV, PIECE), shape(ROWS, PIECE)),
        in_specs=[pl.BlockSpec(memory_space=pltpu.SMEM), vmem(), vmem()],
        out_specs=(vmem(),) * 2,
        scratch_shapes=[scratch(NLEV * NLEV * 8, LANES)],
        compiler_params=params(32),
        name="remap",
    )(level_weights, first, second)
    return jnp.transpose(remapped, (0, 2, 1, 3)), column_mass


def solution(mesh):
    placed = (
        P(None, "lev", "lat", None),
        P("lev", "lat", None),
        P("lev", "lat", None),
        P("lev", "lat", None),
        P(),
    )
    return jax.shard_map(
        local,
        mesh=mesh,
        in_specs=placed,
        out_specs=(P(None, None, "lat", "lev"), P("lat", "lev")),
        check_vma=False,
    )
```

```python
import math

import jax
import jax.numpy as jnp
import ml_dtypes
import numpy as np
from jax import lax
from jax.experimental import pallas as pl
from jax.experimental.pallas import tpu as pltpu
from jax.sharding import PartitionSpec as P

NT = 8
NLEV = 8
NLAT = 768
NLON = 1152
ROWS = 12
LANES = 128
CHUNKS = NLON // LANES
PIECE = NLON // NLEV
TAIL = PIECE - LANES
HALO = 3
INNER = tuple(range(HALO, ROWS - HALO))
OUTER = tuple(range(HALO)) + tuple(range(ROWS - HALO, ROWS))
HALF = ROWS // 2
MSG = 64
SEND = 256
ZFLOPS = 2 * 10**10
ZBYTES = 10**10
WHOLE = 62
RFLOPS = 10000000000
F32 = jnp.float32
BF16 = jnp.bfloat16


def vmem():
    return pl.BlockSpec(memory_space=pltpu.VMEM)


def far():
    return pl.BlockSpec(memory_space=pltpu.HBM)


def copies(semaphores, *pairs):
    return [
        pltpu.make_async_copy(source, target, semaphores.at[i])
        for i, (source, target) in enumerate(pairs)
    ]


def params(mib):
    return pltpu.CompilerParams(vmem_limit_bytes=mib * 1024 * 1024)


def shifted(x, d):
    return x if d == 0 else pltpu.roll(x, (-d) % NLON, 1)


def face_coefs(courant):
    m = jnp.abs(courant)
    k = m * (3.0 - 2.0 * m)
    return 1.0 - 0.5 * (m + k), k, 0.5 * (m - k), courant > 0.0


def flux_stencil(mass, n, k, w, positive):
    zero = jnp.zeros_like(mass)
    a, b, c = mass * n, mass * k, mass * w
    bp, cp = jnp.where(positive, b, zero), jnp.where(positive, c, zero)
    bm, cm = b - bp, c - cp
    s, t = 7.0 / 12.0, 1.0 / 12.0
    return (
        -t * cp,
        s * cp - t * a,
        s * (a + cp) - t * cm + bp,
        s * (a + cm) - t * cp + bm,
        s * cm - t * a,
        -t * cm,
    )


def divergence_stencil(faces, ahead):
    nxt = [ahead(f) for f in faces]
    return (
        [-faces[0]] + [nxt[i] - faces[i + 1] for i in range(5)] + [nxt[5]]
    )


def meridional(band, hx, cy, e_scr, base, store):
    first = (band * ROWS).astype(F32)
    ids = first + lax.broadcasted_iota(jnp.int32, (16, LANES), 0).astype(F32)
    centre = jnp.sin(math.pi * (ids + 0.5) / NLAT)[:, :1]
    face_cos = jnp.sin(math.pi * ids / NLAT)[:, :1]
    e_scr[0:16] = (7.0 / 12.0) * (hx[1:17] + hx[2:18]) - (1.0 / 12.0) * (hx[0:16] + hx[3:19])
    e_scr[16:24] = jnp.zeros((8, NLON), F32)
    c = cy[...]
    n, k, w, positive = face_coefs(c)
    cell = jnp.where(positive, hx[2:18], hx[3:19])
    far = jnp.where(positive, e_scr[0:16], e_scr[2:18])
    mass = c * face_cos * (n * e_scr[1:17] + k * cell + w * far)
    faces = flux_stencil(mass, n, k, w, positive)

    def ahead(x):
        return pltpu.roll(x, 15, 0)

    stencil = divergence_stencil(faces, ahead)
    per_centre = 1.0 / centre
    new_thick = base - (ahead(mass) - mass) * per_centre
    inverse = 1.0 / new_thick
    scale = inverse * per_centre
    for d in range(7):
        weight = -stencil[d] * scale
        if d == 3:
            weight = weight + hx[3:19] * inverse
        store[d] = weight
    store[7] = -inverse
    return new_thick


def row_of(ref, index, row):
    return jnp.broadcast_to(ref[index, row : row + 1, :], (NT, NLON))


def lane_ids(rows=NT):
    return lax.broadcasted_iota(jnp.int32, (rows, LANES), 1)


def turn(x, amount):
    amount %= LANES
    return x if amount == 0 else pltpu.roll(x, amount, 1)


def window(lanes, low, high, dest):
    if dest == 0:
        return low
    keep = lanes < LANES - TAIL * dest
    return jnp.where(keep, turn(low, -TAIL * dest), turn(high, -TAIL * dest))


def pack_message(rows, ratio_row, new_thick, msg):
    lanes = lane_ids()
    tails = [jnp.zeros((NT, LANES), F32)] * NLEV
    for v, r in enumerate(rows):
        ratio = ratio_row(r)
        part = [ratio[:, LANES * c : LANES * (c + 1)] for c in range(CHUNKS)]
        here = (lanes >= TAIL * v) & (lanes < TAIL * (v + 1))
        for dest in range(NLEV):
            msg[dest, 8 * v : 8 * v + 8, :] = window(lanes, part[dest], part[dest + 1], dest)
            tails[dest] = jnp.where(here, turn(part[dest + 1], TAIL * (v - dest)), tails[dest])
    for dest in range(NLEV):
        msg[dest, 8 * HALF : 8 * HALF + 8, :] = tails[dest]
    lanes16 = lane_ids(16)
    wide = lane_ids(1)
    base = 8 * HALF + 8
    for dest in range(NLEV):
        low = new_thick[:, LANES * dest : LANES * (dest + 1)]
        high = new_thick[:, LANES * (dest + 1) : LANES * (dest + 2)]
        main = window(lanes16, low, high, dest)
        last = jnp.ones((1, LANES), F32)
        for v, r in enumerate(rows):
            msg[dest, base + v : base + v + 1, :] = main[r : r + 1]
            here = (wide >= TAIL * v) & (wide < TAIL * (v + 1))
            last = jnp.where(here, turn(high[r : r + 1], TAIL * (v - dest)), last)
        msg[dest, base + HALF : base + HALF + 1, :] = last
        msg[dest, base + HALF + 1 : base + HALF + 2, :] = jnp.ones((1, LANES), F32)


def tracer_tile(ref, row, chunk):
    return ref[pl.ds(CHUNKS * row + chunk, NT, stride=CHUNKS * ROWS), :]


def put_edge(ref, first, q_ref, h_ref, cy_ref):
    for i in range(HALO):
        for c in range(CHUNKS):
            at = 8 * (CHUNKS * i + c)
            ref[at : at + 8, :] = tracer_tile(q_ref, first + i, c)
    at = 8 * CHUNKS * HALO
    size = CHUNKS * HALO
    for i in range(size):
        ref[at + i : at + i + 1, :] = h_ref[CHUNKS * first + i]
    for i in range(CHUNKS):
        ref[at + size + i : at + size + i + 1, :] = cy_ref[i]
    ref[at + size + CHUNKS : SEND, :] = jnp.zeros((SEND - at - size - CHUNKS, LANES), F32)


def split_bf16(x):
    high = x.astype(BF16)
    return high, (x - high.astype(F32)).astype(BF16)


def dot_parts(x, basis_high, basis_low, dims):
    high, low = split_bf16(x)
    rows = x.shape[0]
    both = lax.dot_general(
        jnp.concatenate([high, low], axis=0), basis_high, dims, preferred_element_type=F32
    )
    small = lax.dot_general(high, basis_low, dims, preferred_element_type=F32)
    return both[:rows] + both[rows:] + small


FORWARD = (((1,), (0,)), ((), ()))
BACKWARD = (((1,), (1,)), ((), ()))


def filter_tables():
    b = np.arange(LANES)
    m = np.arange(LANES)
    blocks = []
    for s in range(1, 5):
        angle = 2.0 * np.pi * ((b[:, None] * (CHUNKS * m[None] + s)) % NLON) / NLON
        cos, sin = np.cos(angle), np.sin(angle)
        blocks.append(np.block([[cos, -sin], [sin, cos]]))
    angle = 2.0 * np.pi * ((b[:, None] * m[None]) % LANES) / LANES
    zero = np.where(m[None] <= LANES // 2, np.cos(angle), np.sin(angle))
    wide = np.stack(blocks)

    def halves(x):
        high = x.astype(np.float32).astype(ml_dtypes.bfloat16)
        low = (x - high.astype(np.float64)).astype(np.float32).astype(ml_dtypes.bfloat16)
        return np.stack([high, low])

    waves = np.concatenate([CHUNKS * m + s for s in range(5)])
    sines = np.sin(np.pi * waves / NLON)
    limit = np.where(waves == 0, 1e30, 4.0 / np.where(waves == 0, 1.0, sines * sines))
    weight = np.full(waves.shape, 2.0 / NLON)
    weight[0] = 1.0 / NLON
    weight[LANES // 2] = 1.0 / NLON
    table = np.zeros((8, waves.size), np.float32)
    table[0], table[1] = limit, weight
    return halves(wide), halves(zero), table


def smooth(band, rows, z_scr, spec_scr, wide_ref, zero_ref, table_ref):
    first = (band * ROWS).astype(F32)
    ids = first + lax.broadcasted_iota(jnp.int32, (16, LANES), 0).astype(F32)
    centre = jnp.sin(math.pi * (ids + 0.5) / NLAT)[:, :1]
    damping = jnp.minimum(1.0, centre * centre * table_ref[0:1, :]) * table_ref[1:2, :]
    x = [z_scr[:, LANES * a : LANES * (a + 1)] for a in range(CHUNKS)]
    plus = [x[a] + x[CHUNKS - a] for a in range(1, 5)]
    minus = [x[a] - x[CHUNKS - a] for a in range(1, 5)]

    def damp(block):
        blocks = [
            jnp.broadcast_to(damping[r : r + 1, LANES * block : LANES * (block + 1)], (NT, LANES))
            for r in rows
        ]
        return jnp.concatenate(blocks, axis=0)

    total = x[0] + plus[0] + plus[1] + plus[2] + plus[3]
    spectrum = dot_parts(total, zero_ref[0], zero_ref[1], FORWARD) * damp(0)
    spec_scr[:, 0:LANES] = dot_parts(spectrum, zero_ref[0], zero_ref[1], BACKWARD)
    for s in range(1, 5):
        real, imag = x[0], None
        for a in range(1, 5):
            angle = 2.0 * math.pi * (s * a % CHUNKS) / CHUNKS
            real = real + plus[a - 1] * math.cos(angle)
            term = minus[a - 1] * -math.sin(angle)
            imag = term if imag is None else imag + term
        spectrum = dot_parts(
            jnp.concatenate([real, imag], axis=1), wide_ref[0, s - 1], wide_ref[1, s - 1], FORWARD
        )
        factor = damp(s)
        spectrum = spectrum * jnp.concatenate([factor, factor], axis=1)
        at = LANES * (2 * s - 1)
        spec_scr[:, at : at + 2 * LANES] = dot_parts(
            spectrum, wide_ref[0, s - 1], wide_ref[1, s - 1], BACKWARD
        )
    mean = spec_scr[:, 0:LANES]
    real = [spec_scr[:, LANES * (2 * s - 1) : LANES * 2 * s] for s in range(1, 5)]
    imag = [spec_scr[:, LANES * 2 * s : LANES * (2 * s + 1)] for s in range(1, 5)]
    z_scr[:, 0:LANES] = mean + real[0] + real[1] + real[2] + real[3]
    for a in range(1, 5):
        even, odd = mean, None
        for s in range(1, 5):
            angle = 2.0 * math.pi * (s * a % CHUNKS) / CHUNKS
            even = even + real[s - 1] * math.cos(angle)
            term = imag[s - 1] * math.sin(angle)
            odd = term if odd is None else odd + term
        z_scr[:, LANES * a : LANES * (a + 1)] = even - odd
        b = CHUNKS - a
        z_scr[:, LANES * b : LANES * (b + 1)] = even + odd


def combine(r, weights, q_of, z_row):
    total = row_of(weights, 7, r) * z_row
    for d in range(7):
        total = total + row_of(weights, d, r) * q_of(r + d - HALO)
    return total


def spread(ref, scr, at):
    for r in range(ROWS):
        for c in range(CHUNKS):
            scr[at + r : at + r + 1, LANES * c : LANES * (c + 1)] = ref[CHUNKS * r + c]


def is_polar(band):
    south, north = band * ROWS, NLAT - 1 - (band * ROWS + ROWS - 1)
    return jnp.minimum(south, north) < NLAT // 6


def zonal(rows, q_in, h_in, cx_in, cx_scr, hx_scr, wx_scr, z_scr, smooth_rows):
    band = lax.axis_index("lat")
    hx_scr[...] = jnp.zeros(hx_scr.shape, F32)
    spread(h_in, hx_scr, HALO)
    spread(cx_in, cx_scr, 0)
    cx_scr[ROWS:16] = jnp.zeros((4, NLON), F32)
    h = hx_scr[HALO : HALO + 16]
    c = cx_scr[...]
    n, k, w, positive = face_coefs(c)
    west = shifted(h, -1)
    edge = (7.0 / 12.0) * (west + h) - (1.0 / 12.0) * (shifted(h, -2) + shifted(h, 1))
    far = jnp.where(positive, shifted(edge, -1), shifted(edge, 1))
    mass = c * (n * edge + k * jnp.where(positive, west, h) + w * far)
    faces = flux_stencil(mass, n, k, w, positive)
    stencil = divergence_stencil(faces, lambda f: shifted(f, 1))
    for d in range(7):
        wx_scr[d] = stencil[d]
    for v, r in enumerate(rows):
        row = tracer_row(q_in, r)
        total = row_of(wx_scr, 3, r) * row
        for d in (-3, -2, -1, 1, 2, 3):
            total = total + row_of(wx_scr, d + 3, r) * shifted(row, d)
        z_scr[NT * v : NT * (v + 1), :] = total

    @pl.when(is_polar(band))
    def _():
        smooth_rows(band)

    return h - (shifted(mass, 1) - mass)


def tracer_row(ref, row):
    return jnp.concatenate([tracer_tile(ref, row, chunk) for chunk in range(CHUNKS)], axis=1)


def is_early(band):
    return band % 4 < 2


def inner_work(band, far_refs, near_refs, msg_far, work, semaphores, loaded):
    msg, cx_scr, hx_scr, cy_scr, e_scr, wx_scr, wy_scr, z_scr, spec_scr, q_scr = work
    q_in, h_in, cy_in, cx_in, wide_ref, zero_ref, table_ref = near_refs
    loads = [
        pltpu.make_async_copy(far_refs[i], near_refs[i], semaphores.at[i]) for i in range(loaded, 7)
    ]
    fields, tables = loads[: 4 - loaded], loads[4 - loaded :]
    for load in fields:
        load.start()

    @pl.when(is_polar(band))
    def _():
        for load in tables:
            load.start()

    for load in fields:
        load.wait()

    def smooth_rows(band):
        for load in tables:
            load.wait()
        smooth(band, INNER, z_scr, spec_scr, wide_ref, zero_ref, table_ref)

    base = zonal(INNER, q_in, h_in, cx_in, cx_scr, hx_scr, wx_scr, z_scr, smooth_rows)
    spread(cy_in, cy_scr, 0)
    cy_scr[ROWS:16] = jnp.zeros((4, NLON), F32)
    new_thick = meridional(band, hx_scr, cy_scr, e_scr, base, wy_scr)
    for r in range(ROWS):
        q_scr[r] = tracer_row(q_in, r)

    def ratio_row(r):
        v = INNER.index(r)
        return combine(r, wy_scr, lambda j: q_scr[j], z_scr[NT * v : NT * (v + 1), :])

    pack_message(INNER, ratio_row, new_thick, msg)
    move = pltpu.make_async_copy(msg, msg_far, semaphores.at[7])
    move.start()
    move.wait()


def edge_kernel(*refs):
    far_refs, (odd_ref, even_ref, msg_far), near_refs = refs[:7], refs[7:10], refs[10:17]
    work, semaphores = refs[17:27], refs[27]
    q_ref, h_ref, cy_ref = near_refs[:3]
    band = lax.axis_index("lat")
    loads = copies(semaphores, *zip(far_refs[:3], near_refs[:3]))
    for load in loads:
        load.start()
    for load in loads:
        load.wait()

    @pl.when(band % 2 == 0)
    def _():
        put_edge(even_ref, ROWS - HALO, q_ref, h_ref, cy_ref)
        put_edge(odd_ref, 0, q_ref, h_ref, cy_ref)

    @pl.when(band % 2 == 1)
    def _():
        put_edge(odd_ref, ROWS - HALO, q_ref, h_ref, cy_ref)
        put_edge(even_ref, 0, q_ref, h_ref, cy_ref)

    @pl.when(is_early(band))
    def _():
        inner_work(band, far_refs, near_refs, msg_far, work, semaphores, 3)


def inner_kernel(*refs):
    far_refs, msg_far, near_refs = refs[:7], refs[10], refs[11:18]
    work, semaphores = refs[18:28], refs[28]
    band = lax.axis_index("lat")

    @pl.when(jnp.logical_not(is_early(band)))
    def _():
        inner_work(band, far_refs, near_refs, msg_far, work, semaphores, 0)


def zonal_kernel(
    q_in, h_in, cx_in, wide_ref, zero_ref, table_ref,
    z_out, base_out,
    cx_scr, hx_scr, wx_scr, spec_scr,
):
    def smooth_rows(band):
        smooth(band, OUTER, z_out, spec_scr, wide_ref, zero_ref, table_ref)

    base_out[...] = zonal(OUTER, q_in, h_in, cx_in, cx_scr, hx_scr, wx_scr, z_out, smooth_rows)


def outer_kernel(
    q_in, z_ref, base_ref, h_in, cy_in, odd_ref, even_ref,
    msg,
    hx_scr, cy_scr, e_scr, wy_scr, q_scr,
):
    band = lax.axis_index("lat")
    spread(h_in, hx_scr, HALO)
    hx_scr[ROWS + 2 * HALO : 24] = jnp.zeros((24 - ROWS - 2 * HALO, NLON), F32)
    spread(cy_in, cy_scr, 0)
    cy_scr[ROWS:16] = jnp.zeros((4, NLON), F32)

    def take(south_ref, north_ref):
        for i in range(HALO):
            for c in range(CHUNKS):
                at = 8 * (CHUNKS * i + c)
                lanes = slice(LANES * c, LANES * (c + 1))
                q_scr[i, :, lanes] = south_ref[at : at + 8, :]
                q_scr[HALO + ROWS + i, :, lanes] = north_ref[at : at + 8, :]
        for c in range(CHUNKS):
            at = 8 * CHUNKS * HALO + c
            lanes = slice(LANES * c, LANES * (c + 1))
            hx_scr[0:HALO, lanes] = south_ref[pl.ds(at, HALO, stride=CHUNKS), :]
            hx_scr[HALO + ROWS : ROWS + 2 * HALO, lanes] = north_ref[pl.ds(at, HALO, stride=CHUNKS), :]
            at = at + CHUNKS * HALO
            cy_scr[ROWS : ROWS + 1, lanes] = north_ref[at : at + 1, :]

    @pl.when(band % 2 == 0)
    def _():
        take(odd_ref, even_ref)

    @pl.when(band % 2 == 1)
    def _():
        take(even_ref, odd_ref)

    new_thick = meridional(band, hx_scr, cy_scr, e_scr, base_ref[...], wy_scr)

    for r in range(ROWS):
        q_scr[HALO + r] = tracer_row(q_in, r)

    def ratio_row(r):
        v = OUTER.index(r)
        return combine(r, wy_scr, lambda j: q_scr[HALO + j], z_ref[NT * v : NT * (v + 1), :])

    pack_message(OUTER, ratio_row, new_thick, msg)


def remap_half(rows, places, weight_ref, in_ref, out_ref, mass_ref, inter_scr):
    weight_sum = weight_ref[0]
    for k in range(1, NLEV):
        weight_sum = weight_sum + weight_ref[k]
    base = 8 * HALF + 8
    thick = [in_ref[i, base : base + 8, :] for i in range(NLEV)]
    upper, lower = [thick[0]], []
    for i in range(1, NLEV):
        upper.append(upper[-1] + thick[i])
    for i in range(NLEV):
        lower.append(upper[i] - thick[i])
    total = upper[-1]
    for v, r in enumerate(rows):
        mass_ref[r : r + 1, 0:LANES] = total[v : v + 1]
        mass_ref[r : r + 1, LANES:PIECE] = turn(total[HALF : HALF + 1], -TAIL * v)[:, :TAIL]
    reach = None
    for k in range(NLEV):
        target = total * (weight_ref[k] / weight_sum)
        reach = target if reach is None else reach + target
        start = reach - target
        scale = 1.0 / target
        for i in range(NLEV):
            overlap = jnp.minimum(upper[i], reach) - jnp.maximum(lower[i], start)
            at = 8 * (NLEV * i + k)
            inter_scr[at : at + 8, :] = jnp.maximum(overlap, 0.0) * scale
    for v in range(HALF + 1):
        moved = [None] * NT
        for i in range(NLEV):
            share = inter_scr[pl.ds(8 * NLEV * i + v, NLEV, stride=8), :]
            for t in range(NT):
                at = 8 * v + t
                term = jnp.broadcast_to(in_ref[i, at : at + 1, :], (NLEV, LANES)) * share
                moved[t] = term if i == 0 else moved[t] + term
        for t in range(NT):
            if v < HALF:
                out_ref[t, places[v], :, 0:LANES] = moved[t]
            else:
                for u in range(HALF):
                    out_ref[t, places[u], :, LANES:PIECE] = turn(moved[t], -TAIL * u)[:, :TAIL]


def inner_remap_kernel(weight_ref, in_ref, out_ref, mass_ref, inter_scr):
    mass_ref[...] = jnp.zeros(mass_ref.shape, F32)
    remap_half(INNER, range(HALF), weight_ref, in_ref, out_ref, mass_ref, inter_scr)


def outer_remap_kernel(weight_ref, in_ref, inner_ref, inner_mass, out_ref, mass_ref, inter_scr):
    mass_ref[...] = inner_mass[...]
    out_ref[:, HALO : ROWS - HALO] = inner_ref[...]
    remap_half(OUTER, OUTER, weight_ref, in_ref, out_ref, mass_ref, inter_scr)


def swaps(first, bands):
    low = range(first, bands - 1, 2)
    return [(i, i + 1) for i in low] + [(i + 1, i) for i in low]


def shape(*dims):
    return jax.ShapeDtypeStruct(dims, F32)


def scratch(*dims):
    return pltpu.VMEM(dims, F32)


def local(tracers, thickness, courant_x, courant_y, level_weights):
    bands = lax.axis_size("lat")
    wide, zero, table = filter_tables()
    q_in = tracers.reshape(NT * ROWS * CHUNKS, LANES)
    h_in, cx_in, cy_in = (
        field.reshape(ROWS * CHUNKS, 1, LANES) for field in (thickness, courant_x, courant_y)
    )
    tables = tuple(jnp.asarray(t) for t in (wide, zero, table))
    operands = (q_in, h_in, cy_in, cx_in, *tables)
    room = (
        [scratch(NT * ROWS * CHUNKS, LANES)]
        + [scratch(ROWS * CHUNKS, 1, LANES)] * 3
        + [pltpu.VMEM(t.shape, t.dtype) for t in tables]
        + [
            scratch(NLEV, MSG, LANES),
            scratch(16, NLON), scratch(24, NLON), scratch(16, NLON), scratch(24, NLON),
            scratch(7, 16, NLON), scratch(8, 16, NLON),
            scratch(HALF * NT, NLON), scratch(HALF * NT, NLON), scratch(ROWS, NT, NLON),
            pltpu.SemaphoreType.DMA((8,)),
        ]
    )
    odd, even, message = pl.pallas_call(
        edge_kernel,
        out_shape=(shape(SEND, LANES),) * 2 + (shape(NLEV, MSG, LANES),),
        in_specs=[far()] * 7,
        out_specs=(vmem(),) * 2 + (far(),),
        scratch_shapes=room,
        compiler_params=params(WHOLE),
        name="edge_rows",
    )(*operands)
    sent = (odd, even)
    odd = lax.ppermute(odd, "lat", swaps(1, bands))
    even = lax.ppermute(even, "lat", swaps(0, bands))
    message = pl.pallas_call(
        inner_kernel,
        out_shape=shape(NLEV, MSG, LANES),
        in_specs=[far()] * 10,
        out_specs=far(),
        scratch_shapes=room,
        input_output_aliases={7: 0},
        compiler_params=params(WHOLE),
        name="inner_rows",
    )(*operands, message, *sent)
    first = message
    first = lax.all_to_all(first, "lev", split_axis=0, concat_axis=0, tiled=True)
    z, base = pl.pallas_call(
        zonal_kernel,
        out_shape=(shape(HALF * NT, NLON), shape(16, NLON)),
        in_specs=[vmem()] * 6,
        out_specs=(vmem(),) * 2,
        scratch_shapes=[
            scratch(16, NLON), scratch(24, NLON), scratch(7, 16, NLON), scratch(HALF * NT, NLON),
        ],
        compiler_params=params(32),
        cost_estimate=pl.CostEstimate(flops=ZFLOPS, bytes_accessed=ZBYTES, transcendentals=0),
        name="outer_zonal",
    )(q_in, h_in, cx_in, *tables)
    second = pl.pallas_call(
        outer_kernel,
        out_shape=shape(NLEV, MSG, LANES),
        in_specs=[vmem()] * 7,
        out_specs=vmem(),
        scratch_shapes=[
            scratch(24, NLON), scratch(16, NLON), scratch(24, NLON), scratch(8, 16, NLON),
            scratch(ROWS + 2 * HALO, NT, NLON),
        ],
        compiler_params=params(32),
        name="outer_rows",
    )(q_in, z, base, h_in, cy_in, odd, even)
    second = lax.all_to_all(second, "lev", split_axis=0, concat_axis=0, tiled=True)
    smem = pl.BlockSpec(memory_space=pltpu.SMEM)
    inner_out, inner_mass = pl.pallas_call(
        inner_remap_kernel,
        out_shape=(shape(NT, HALF, NLEV, PIECE), shape(ROWS, PIECE)),
        in_specs=[smem, vmem()],
        out_specs=(vmem(),) * 2,
        scratch_shapes=[scratch(NLEV * NLEV * 8, LANES)],
        compiler_params=params(32),
        cost_estimate=pl.CostEstimate(flops=RFLOPS, bytes_accessed=RFLOPS, transcendentals=0),
        name="inner_remap",
    )(level_weights, first)
    remapped, column_mass = pl.pallas_call(
        outer_remap_kernel,
        out_shape=(shape(NT, ROWS, NLEV, PIECE), shape(ROWS, PIECE)),
        in_specs=[smem] + [vmem()] * 3,
        out_specs=(vmem(),) * 2,
        scratch_shapes=[scratch(NLEV * NLEV * 8, LANES)],
        compiler_params=params(32),
        name="outer_remap",
    )(level_weights, second, inner_out, inner_mass)
    return jnp.transpose(remapped, (0, 2, 1, 3)), column_mass


def solution(mesh):
    placed = (
        P(None, "lev", "lat", None),
        P("lev", "lat", None),
        P("lev", "lat", None),
        P("lev", "lat", None),
        P(),
    )
    return jax.shard_map(
        local,
        mesh=mesh,
        in_specs=placed,
        out_specs=(P(None, None, "lat", "lev"), P("lat", "lev")),
        check_vma=False,
    )
```

```python
import math

import jax
import jax.numpy as jnp
import ml_dtypes
import numpy as np
from jax import lax
from jax.experimental import pallas as pl
from jax.experimental.pallas import tpu as pltpu
from jax.sharding import PartitionSpec as P

NT = 8
NLEV = 8
NLAT = 768
NLON = 1152
ROWS = 12
LANES = 128
CHUNKS = NLON // LANES
PIECE = NLON // NLEV
TAIL = PIECE - LANES
HALO = 3
INNER = tuple(range(HALO, ROWS - HALO))
OUTER = tuple(range(HALO)) + tuple(range(ROWS - HALO, ROWS))
HALF = ROWS // 2
MSG = 64
SEND = 256
ZFLOPS = 2 * 10**10
ZBYTES = 10**10
WHOLE = 62
F32 = jnp.float32
BF16 = jnp.bfloat16


def vmem():
    return pl.BlockSpec(memory_space=pltpu.VMEM)


def far():
    return pl.BlockSpec(memory_space=pltpu.HBM)


def copies(semaphores, *pairs):
    return [
        pltpu.make_async_copy(source, target, semaphores.at[i])
        for i, (source, target) in enumerate(pairs)
    ]


def params(mib):
    return pltpu.CompilerParams(vmem_limit_bytes=mib * 1024 * 1024)


def shifted(x, d):
    return x if d == 0 else pltpu.roll(x, (-d) % NLON, 1)


def face_coefs(courant):
    m = jnp.abs(courant)
    k = m * (3.0 - 2.0 * m)
    return 1.0 - 0.5 * (m + k), k, 0.5 * (m - k), courant > 0.0


def flux_stencil(mass, n, k, w, positive):
    zero = jnp.zeros_like(mass)
    a, b, c = mass * n, mass * k, mass * w
    bp, cp = jnp.where(positive, b, zero), jnp.where(positive, c, zero)
    bm, cm = b - bp, c - cp
    s, t = 7.0 / 12.0, 1.0 / 12.0
    return (
        -t * cp,
        s * cp - t * a,
        s * (a + cp) - t * cm + bp,
        s * (a + cm) - t * cp + bm,
        s * cm - t * a,
        -t * cm,
    )


def divergence_stencil(faces, ahead):
    nxt = [ahead(f) for f in faces]
    return (
        [-faces[0]] + [nxt[i] - faces[i + 1] for i in range(5)] + [nxt[5]]
    )


def meridional(band, hx, cy, e_scr, base, store):
    first = (band * ROWS).astype(F32)
    ids = first + lax.broadcasted_iota(jnp.int32, (16, LANES), 0).astype(F32)
    centre = jnp.sin(math.pi * (ids + 0.5) / NLAT)[:, :1]
    face_cos = jnp.sin(math.pi * ids / NLAT)[:, :1]
    e_scr[0:16] = (7.0 / 12.0) * (hx[1:17] + hx[2:18]) - (1.0 / 12.0) * (hx[0:16] + hx[3:19])
    e_scr[16:24] = jnp.zeros((8, NLON), F32)
    c = cy[...]
    n, k, w, positive = face_coefs(c)
    cell = jnp.where(positive, hx[2:18], hx[3:19])
    far = jnp.where(positive, e_scr[0:16], e_scr[2:18])
    mass = c * face_cos * (n * e_scr[1:17] + k * cell + w * far)
    faces = flux_stencil(mass, n, k, w, positive)

    def ahead(x):
        return pltpu.roll(x, 15, 0)

    stencil = divergence_stencil(faces, ahead)
    per_centre = 1.0 / centre
    new_thick = base - (ahead(mass) - mass) * per_centre
    inverse = 1.0 / new_thick
    scale = inverse * per_centre
    for d in range(7):
        weight = -stencil[d] * scale
        if d == 3:
            weight = weight + hx[3:19] * inverse
        store[d] = weight
    store[7] = -inverse
    return new_thick


def row_of(ref, index, row):
    return jnp.broadcast_to(ref[index, row : row + 1, :], (NT, NLON))


def lane_ids(rows=NT):
    return lax.broadcasted_iota(jnp.int32, (rows, LANES), 1)


def turn(x, amount):
    amount %= LANES
    return x if amount == 0 else pltpu.roll(x, amount, 1)


def window(lanes, low, high, dest):
    if dest == 0:
        return low
    keep = lanes < LANES - TAIL * dest
    return jnp.where(keep, turn(low, -TAIL * dest), turn(high, -TAIL * dest))


def pack_message(rows, ratio_row, new_thick, msg):
    lanes = lane_ids()
    tails = [jnp.zeros((NT, LANES), F32)] * NLEV
    for v, r in enumerate(rows):
        ratio = ratio_row(r)
        part = [ratio[:, LANES * c : LANES * (c + 1)] for c in range(CHUNKS)]
        here = (lanes >= TAIL * v) & (lanes < TAIL * (v + 1))
        for dest in range(NLEV):
            msg[dest, 8 * v : 8 * v + 8, :] = window(lanes, part[dest], part[dest + 1], dest)
            tails[dest] = jnp.where(here, turn(part[dest + 1], TAIL * (v - dest)), tails[dest])
    for dest in range(NLEV):
        msg[dest, 8 * HALF : 8 * HALF + 8, :] = tails[dest]
    lanes16 = lane_ids(16)
    wide = lane_ids(1)
    base = 8 * HALF + 8
    for dest in range(NLEV):
        low = new_thick[:, LANES * dest : LANES * (dest + 1)]
        high = new_thick[:, LANES * (dest + 1) : LANES * (dest + 2)]
        main = window(lanes16, low, high, dest)
        last = jnp.ones((1, LANES), F32)
        for v, r in enumerate(rows):
            msg[dest, base + v : base + v + 1, :] = main[r : r + 1]
            here = (wide >= TAIL * v) & (wide < TAIL * (v + 1))
            last = jnp.where(here, turn(high[r : r + 1], TAIL * (v - dest)), last)
        msg[dest, base + HALF : base + HALF + 1, :] = last
        msg[dest, base + HALF + 1 : base + HALF + 2, :] = jnp.ones((1, LANES), F32)


def tracer_tile(ref, row, chunk):
    return ref[pl.ds(CHUNKS * row + chunk, NT, stride=CHUNKS * ROWS), :]


def edge_kernel(
    q_in, h_in, cy_in,
    odd_far, even_far,
    q_ref, h_ref, cy_ref, odd_ref, even_ref, semaphores, out_semaphores,
):
    band = lax.axis_index("lat")
    loads = copies(semaphores, (q_in, q_ref), (h_in, h_ref), (cy_in, cy_ref))
    for load in loads:
        load.start()
    for load in loads:
        load.wait()

    def put(ref, first):
        for i in range(HALO):
            for c in range(CHUNKS):
                at = 8 * (CHUNKS * i + c)
                ref[at : at + 8, :] = tracer_tile(q_ref, first + i, c)
        at = 8 * CHUNKS * HALO
        size = CHUNKS * HALO
        for i in range(size):
            ref[at + i : at + i + 1, :] = h_ref[CHUNKS * first + i]
        for i in range(CHUNKS):
            ref[at + size + i : at + size + i + 1, :] = cy_ref[i]
        ref[at + size + CHUNKS : SEND, :] = jnp.zeros((SEND - at - size - CHUNKS, LANES), F32)

    stores = copies(out_semaphores, (odd_ref, odd_far), (even_ref, even_far))
    for parity, ref, store in ((0, odd_ref, stores[0]), (1, even_ref, stores[1])):
        @pl.when(band % 2 == parity)
        def _(ref=ref):
            put(ref, 0)

        @pl.when(band % 2 != parity)
        def _(ref=ref):
            put(ref, ROWS - HALO)

        store.start()
    for store in stores:
        store.wait()


def split_bf16(x):
    high = x.astype(BF16)
    return high, (x - high.astype(F32)).astype(BF16)


def dot_parts(x, basis_high, basis_low, dims):
    high, low = split_bf16(x)
    rows = x.shape[0]
    both = lax.dot_general(
        jnp.concatenate([high, low], axis=0), basis_high, dims, preferred_element_type=F32
    )
    small = lax.dot_general(high, basis_low, dims, preferred_element_type=F32)
    return both[:rows] + both[rows:] + small


FORWARD = (((1,), (0,)), ((), ()))
BACKWARD = (((1,), (1,)), ((), ()))


def filter_tables():
    b = np.arange(LANES)
    m = np.arange(LANES)
    blocks = []
    for s in range(1, 5):
        angle = 2.0 * np.pi * ((b[:, None] * (CHUNKS * m[None] + s)) % NLON) / NLON
        cos, sin = np.cos(angle), np.sin(angle)
        blocks.append(np.block([[cos, -sin], [sin, cos]]))
    angle = 2.0 * np.pi * ((b[:, None] * m[None]) % LANES) / LANES
    zero = np.where(m[None] <= LANES // 2, np.cos(angle), np.sin(angle))
    wide = np.stack(blocks)

    def halves(x):
        high = x.astype(np.float32).astype(ml_dtypes.bfloat16)
        low = (x - high.astype(np.float64)).astype(np.float32).astype(ml_dtypes.bfloat16)
        return np.stack([high, low])

    waves = np.concatenate([CHUNKS * m + s for s in range(5)])
    sines = np.sin(np.pi * waves / NLON)
    limit = np.where(waves == 0, 1e30, 4.0 / np.where(waves == 0, 1.0, sines * sines))
    weight = np.full(waves.shape, 2.0 / NLON)
    weight[0] = 1.0 / NLON
    weight[LANES // 2] = 1.0 / NLON
    table = np.zeros((8, waves.size), np.float32)
    table[0], table[1] = limit, weight
    return halves(wide), halves(zero), table


def smooth(band, rows, z_scr, spec_scr, wide_ref, zero_ref, table_ref):
    first = (band * ROWS).astype(F32)
    ids = first + lax.broadcasted_iota(jnp.int32, (16, LANES), 0).astype(F32)
    centre = jnp.sin(math.pi * (ids + 0.5) / NLAT)[:, :1]
    damping = jnp.minimum(1.0, centre * centre * table_ref[0:1, :]) * table_ref[1:2, :]
    x = [z_scr[:, LANES * a : LANES * (a + 1)] for a in range(CHUNKS)]
    plus = [x[a] + x[CHUNKS - a] for a in range(1, 5)]
    minus = [x[a] - x[CHUNKS - a] for a in range(1, 5)]

    def damp(block):
        blocks = [
            jnp.broadcast_to(damping[r : r + 1, LANES * block : LANES * (block + 1)], (NT, LANES))
            for r in rows
        ]
        return jnp.concatenate(blocks, axis=0)

    total = x[0] + plus[0] + plus[1] + plus[2] + plus[3]
    spectrum = dot_parts(total, zero_ref[0], zero_ref[1], FORWARD) * damp(0)
    spec_scr[:, 0:LANES] = dot_parts(spectrum, zero_ref[0], zero_ref[1], BACKWARD)
    for s in range(1, 5):
        real, imag = x[0], None
        for a in range(1, 5):
            angle = 2.0 * math.pi * (s * a % CHUNKS) / CHUNKS
            real = real + plus[a - 1] * math.cos(angle)
            term = minus[a - 1] * -math.sin(angle)
            imag = term if imag is None else imag + term
        spectrum = dot_parts(
            jnp.concatenate([real, imag], axis=1), wide_ref[0, s - 1], wide_ref[1, s - 1], FORWARD
        )
        factor = damp(s)
        spectrum = spectrum * jnp.concatenate([factor, factor], axis=1)
        at = LANES * (2 * s - 1)
        spec_scr[:, at : at + 2 * LANES] = dot_parts(
            spectrum, wide_ref[0, s - 1], wide_ref[1, s - 1], BACKWARD
        )
    mean = spec_scr[:, 0:LANES]
    real = [spec_scr[:, LANES * (2 * s - 1) : LANES * 2 * s] for s in range(1, 5)]
    imag = [spec_scr[:, LANES * 2 * s : LANES * (2 * s + 1)] for s in range(1, 5)]
    z_scr[:, 0:LANES] = mean + real[0] + real[1] + real[2] + real[3]
    for a in range(1, 5):
        even, odd = mean, None
        for s in range(1, 5):
            angle = 2.0 * math.pi * (s * a % CHUNKS) / CHUNKS
            even = even + real[s - 1] * math.cos(angle)
            term = imag[s - 1] * math.sin(angle)
            odd = term if odd is None else odd + term
        z_scr[:, LANES * a : LANES * (a + 1)] = even - odd
        b = CHUNKS - a
        z_scr[:, LANES * b : LANES * (b + 1)] = even + odd


def combine(r, weights, q_of, z_row):
    total = row_of(weights, 7, r) * z_row
    for d in range(7):
        total = total + row_of(weights, d, r) * q_of(r + d - HALO)
    return total


def spread(ref, scr, at):
    for r in range(ROWS):
        for c in range(CHUNKS):
            scr[at + r : at + r + 1, LANES * c : LANES * (c + 1)] = ref[CHUNKS * r + c]


def is_polar(band):
    south, north = band * ROWS, NLAT - 1 - (band * ROWS + ROWS - 1)
    return jnp.minimum(south, north) < NLAT // 6


def zonal(rows, q_in, h_in, cx_in, cx_scr, hx_scr, wx_scr, z_scr, smooth_rows):
    band = lax.axis_index("lat")
    hx_scr[...] = jnp.zeros(hx_scr.shape, F32)
    spread(h_in, hx_scr, HALO)
    spread(cx_in, cx_scr, 0)
    cx_scr[ROWS:16] = jnp.zeros((4, NLON), F32)
    h = hx_scr[HALO : HALO + 16]
    c = cx_scr[...]
    n, k, w, positive = face_coefs(c)
    west = shifted(h, -1)
    edge = (7.0 / 12.0) * (west + h) - (1.0 / 12.0) * (shifted(h, -2) + shifted(h, 1))
    far = jnp.where(positive, shifted(edge, -1), shifted(edge, 1))
    mass = c * (n * edge + k * jnp.where(positive, west, h) + w * far)
    faces = flux_stencil(mass, n, k, w, positive)
    stencil = divergence_stencil(faces, lambda f: shifted(f, 1))
    for d in range(7):
        wx_scr[d] = stencil[d]
    for v, r in enumerate(rows):
        row = tracer_row(q_in, r)
        total = row_of(wx_scr, 3, r) * row
        for d in (-3, -2, -1, 1, 2, 3):
            total = total + row_of(wx_scr, d + 3, r) * shifted(row, d)
        z_scr[NT * v : NT * (v + 1), :] = total

    @pl.when(is_polar(band))
    def _():
        smooth_rows(band)

    return h - (shifted(mass, 1) - mass)


def tracer_row(ref, row):
    return jnp.concatenate([tracer_tile(ref, row, chunk) for chunk in range(CHUNKS)], axis=1)


def inner_kernel(
    q_far, h_far, cx_far, cy_far, wide_far, zero_far, table_far, _odd, _even,
    msg,
    cx_scr, hx_scr, cy_scr, e_scr, wx_scr, wy_scr, z_scr, spec_scr, q_scr,
    q_in, h_in, cx_in, cy_in, wide_ref, zero_ref, table_ref, semaphores,
):
    band = lax.axis_index("lat")
    *fields, wide_load, zero_load, table_load = copies(
        semaphores, (q_far, q_in), (h_far, h_in), (cx_far, cx_in), (cy_far, cy_in),
        (wide_far, wide_ref), (zero_far, zero_ref), (table_far, table_ref),
    )
    loads = (wide_load, zero_load, table_load)
    for load in fields:
        load.start()

    @pl.when(is_polar(band))
    def _():
        for load in loads:
            load.start()

    def smooth_rows(band):
        for load in loads:
            load.wait()
        smooth(band, INNER, z_scr, spec_scr, wide_ref, zero_ref, table_ref)

    for load in fields:
        load.wait()
    base = zonal(INNER, q_in, h_in, cx_in, cx_scr, hx_scr, wx_scr, z_scr, smooth_rows)
    spread(cy_in, cy_scr, 0)
    cy_scr[ROWS:16] = jnp.zeros((4, NLON), F32)
    new_thick = meridional(band, hx_scr, cy_scr, e_scr, base, wy_scr)
    for r in range(ROWS):
        q_scr[r] = tracer_row(q_in, r)

    def ratio_row(r):
        v = INNER.index(r)
        return combine(r, wy_scr, lambda j: q_scr[j], z_scr[NT * v : NT * (v + 1), :])

    pack_message(INNER, ratio_row, new_thick, msg)


def zonal_kernel(
    q_in, h_in, cx_in, wide_ref, zero_ref, table_ref,
    z_out, base_out,
    cx_scr, hx_scr, wx_scr, spec_scr,
):
    def smooth_rows(band):
        smooth(band, OUTER, z_out, spec_scr, wide_ref, zero_ref, table_ref)

    base_out[...] = zonal(OUTER, q_in, h_in, cx_in, cx_scr, hx_scr, wx_scr, z_out, smooth_rows)


def outer_kernel(
    q_in, z_ref, base_ref, h_in, cy_in, odd_ref, even_ref,
    msg,
    hx_scr, cy_scr, e_scr, wy_scr, q_scr,
):
    band = lax.axis_index("lat")
    spread(h_in, hx_scr, HALO)
    hx_scr[ROWS + 2 * HALO : 24] = jnp.zeros((24 - ROWS - 2 * HALO, NLON), F32)
    spread(cy_in, cy_scr, 0)
    cy_scr[ROWS:16] = jnp.zeros((4, NLON), F32)

    def take(south_ref, north_ref):
        for i in range(HALO):
            for c in range(CHUNKS):
                at = 8 * (CHUNKS * i + c)
                lanes = slice(LANES * c, LANES * (c + 1))
                q_scr[i, :, lanes] = south_ref[at : at + 8, :]
                q_scr[HALO + ROWS + i, :, lanes] = north_ref[at : at + 8, :]
        for c in range(CHUNKS):
            at = 8 * CHUNKS * HALO + c
            lanes = slice(LANES * c, LANES * (c + 1))
            hx_scr[0:HALO, lanes] = south_ref[pl.ds(at, HALO, stride=CHUNKS), :]
            hx_scr[HALO + ROWS : ROWS + 2 * HALO, lanes] = north_ref[pl.ds(at, HALO, stride=CHUNKS), :]
            at = at + CHUNKS * HALO
            cy_scr[ROWS : ROWS + 1, lanes] = north_ref[at : at + 1, :]

    @pl.when(band % 2 == 0)
    def _():
        take(odd_ref, even_ref)

    @pl.when(band % 2 == 1)
    def _():
        take(even_ref, odd_ref)

    new_thick = meridional(band, hx_scr, cy_scr, e_scr, base_ref[...], wy_scr)

    for r in range(ROWS):
        q_scr[HALO + r] = tracer_row(q_in, r)

    def ratio_row(r):
        v = OUTER.index(r)
        return combine(r, wy_scr, lambda j: q_scr[HALO + j], z_ref[NT * v : NT * (v + 1), :])

    pack_message(OUTER, ratio_row, new_thick, msg)


def remap_kernel(weight_ref, first_ref, second_ref, out_ref, mass_ref, inter_scr):
    weight_sum = weight_ref[0]
    for k in range(1, NLEV):
        weight_sum = weight_sum + weight_ref[k]
    base = 8 * HALF + 8
    for in_ref, rows in ((first_ref, INNER), (second_ref, OUTER)):
        thick = [in_ref[i, base : base + 8, :] for i in range(NLEV)]
        upper, lower = [thick[0]], []
        for i in range(1, NLEV):
            upper.append(upper[-1] + thick[i])
        for i in range(NLEV):
            lower.append(upper[i] - thick[i])
        total = upper[-1]
        for v, r in enumerate(rows):
            mass_ref[r : r + 1, 0:LANES] = total[v : v + 1]
            mass_ref[r : r + 1, LANES:PIECE] = turn(total[HALF : HALF + 1], -TAIL * v)[:, :TAIL]
        reach = None
        for k in range(NLEV):
            target = total * (weight_ref[k] / weight_sum)
            reach = target if reach is None else reach + target
            start = reach - target
            scale = 1.0 / target
            for i in range(NLEV):
                overlap = jnp.minimum(upper[i], reach) - jnp.maximum(lower[i], start)
                at = 8 * (NLEV * i + k)
                inter_scr[at : at + 8, :] = jnp.maximum(overlap, 0.0) * scale
        for v in range(HALF + 1):
            moved = [None] * NT
            for i in range(NLEV):
                share = inter_scr[pl.ds(8 * NLEV * i + v, NLEV, stride=8), :]
                for t in range(NT):
                    at = 8 * v + t
                    term = jnp.broadcast_to(in_ref[i, at : at + 1, :], (NLEV, LANES)) * share
                    moved[t] = term if i == 0 else moved[t] + term
            for t in range(NT):
                if v < HALF:
                    out_ref[t, rows[v], :, 0:LANES] = moved[t]
                else:
                    for u, r in enumerate(rows):
                        out_ref[t, r, :, LANES:PIECE] = turn(moved[t], -TAIL * u)[:, :TAIL]


def swaps(first, bands):
    low = range(first, bands - 1, 2)
    return [(i, i + 1) for i in low] + [(i + 1, i) for i in low]


def shape(*dims):
    return jax.ShapeDtypeStruct(dims, F32)


def scratch(*dims):
    return pltpu.VMEM(dims, F32)


def local(tracers, thickness, courant_x, courant_y, level_weights):
    bands = lax.axis_size("lat")
    wide, zero, table = filter_tables()
    q_in = tracers.reshape(NT * ROWS * CHUNKS, LANES)
    h_in, cx_in, cy_in = (
        field.reshape(ROWS * CHUNKS, 1, LANES) for field in (thickness, courant_x, courant_y)
    )
    odd, even = pl.pallas_call(
        edge_kernel,
        out_shape=(shape(SEND, LANES),) * 2,
        in_specs=[far()] * 3,
        out_specs=(far(),) * 2,
        scratch_shapes=[
            scratch(NT * ROWS * CHUNKS, LANES), scratch(ROWS * CHUNKS, 1, LANES),
            scratch(ROWS * CHUNKS, 1, LANES), scratch(SEND, LANES), scratch(SEND, LANES),
            pltpu.SemaphoreType.DMA((3,)), pltpu.SemaphoreType.DMA((2,)),
        ],
        compiler_params=params(WHOLE),
        name="edge_rows",
    )(q_in, h_in, cy_in)
    sent = (odd, even)
    odd = lax.ppermute(odd, "lat", swaps(1, bands))
    even = lax.ppermute(even, "lat", swaps(0, bands))
    tables = (jnp.asarray(wide), jnp.asarray(zero), jnp.asarray(table))
    first = pl.pallas_call(
        inner_kernel,
        out_shape=shape(NLEV, MSG, LANES),
        in_specs=[far()] * 9,
        out_specs=vmem(),
        scratch_shapes=[
            scratch(16, NLON), scratch(24, NLON), scratch(16, NLON), scratch(24, NLON),
            scratch(7, 16, NLON), scratch(8, 16, NLON),
            scratch(HALF * NT, NLON), scratch(HALF * NT, NLON), scratch(ROWS, NT, NLON),
            scratch(NT * ROWS * CHUNKS, LANES),
        ]
        + [scratch(ROWS * CHUNKS, 1, LANES)] * 3
        + [pltpu.VMEM(t.shape, t.dtype) for t in tables]
        + [pltpu.SemaphoreType.DMA((7,))],
        compiler_params=params(WHOLE),
        name="inner_rows",
    )(q_in, h_in, cx_in, cy_in, *tables, *sent)
    first = lax.all_to_all(first, "lev", split_axis=0, concat_axis=0, tiled=True)
    z, base = pl.pallas_call(
        zonal_kernel,
        out_shape=(shape(HALF * NT, NLON), shape(16, NLON)),
        in_specs=[vmem()] * 6,
        out_specs=(vmem(),) * 2,
        scratch_shapes=[
            scratch(16, NLON), scratch(24, NLON), scratch(7, 16, NLON), scratch(HALF * NT, NLON),
        ],
        compiler_params=params(32),
        cost_estimate=pl.CostEstimate(flops=ZFLOPS, bytes_accessed=ZBYTES, transcendentals=0),
        name="outer_zonal",
    )(q_in, h_in, cx_in, *tables)
    second = pl.pallas_call(
        outer_kernel,
        out_shape=shape(NLEV, MSG, LANES),
        in_specs=[vmem()] * 7,
        out_specs=vmem(),
        scratch_shapes=[
            scratch(24, NLON), scratch(16, NLON), scratch(24, NLON), scratch(8, 16, NLON),
            scratch(ROWS + 2 * HALO, NT, NLON),
        ],
        compiler_params=params(32),
        name="outer_rows",
    )(q_in, z, base, h_in, cy_in, odd, even)
    second = lax.all_to_all(second, "lev", split_axis=0, concat_axis=0, tiled=True)
    remapped, column_mass = pl.pallas_call(
        remap_kernel,
        out_shape=(shape(NT, ROWS, NLEV, PIECE), shape(ROWS, PIECE)),
        in_specs=[pl.BlockSpec(memory_space=pltpu.SMEM), vmem(), vmem()],
        out_specs=(vmem(),) * 2,
        scratch_shapes=[scratch(NLEV * NLEV * 8, LANES)],
        compiler_params=params(32),
        name="remap",
    )(level_weights, first, second)
    return jnp.transpose(remapped, (0, 2, 1, 3)), column_mass


def solution(mesh):
    placed = (
        P(None, "lev", "lat", None),
        P("lev", "lat", None),
        P("lev", "lat", None),
        P("lev", "lat", None),
        P(),
    )
    return jax.shard_map(
        local,
        mesh=mesh,
        in_specs=placed,
        out_specs=(P(None, None, "lat", "lev"), P("lat", "lev")),
        check_vma=False,
    )
```

```python
import math

import jax
import jax.numpy as jnp
import ml_dtypes
import numpy as np
from jax import lax
from jax.experimental import pallas as pl
from jax.experimental.pallas import tpu as pltpu
from jax.sharding import PartitionSpec as P

NT = 8
NLEV = 8
NLAT = 768
NLON = 1152
ROWS = 12
LANES = 128
CHUNKS = NLON // LANES
PIECE = NLON // NLEV
TAIL = PIECE - LANES
HALO = 3
INNER = tuple(range(HALO, ROWS - HALO))
OUTER = tuple(range(HALO)) + tuple(range(ROWS - HALO, ROWS))
HALF = ROWS // 2
MSG = 64
SEND = 256
ZFLOPS = 2 * 10**10
ZBYTES = 10**10
WHOLE = 62
F32 = jnp.float32
BF16 = jnp.bfloat16


def vmem():
    return pl.BlockSpec(memory_space=pltpu.VMEM)


def far():
    return pl.BlockSpec(memory_space=pltpu.HBM)


def copies(semaphores, *pairs):
    return [
        pltpu.make_async_copy(source, target, semaphores.at[i])
        for i, (source, target) in enumerate(pairs)
    ]


def params(mib):
    return pltpu.CompilerParams(vmem_limit_bytes=mib * 1024 * 1024)


def shifted(x, d):
    return x if d == 0 else pltpu.roll(x, (-d) % NLON, 1)


def face_coefs(courant):
    m = jnp.abs(courant)
    k = m * (3.0 - 2.0 * m)
    return 1.0 - 0.5 * (m + k), k, 0.5 * (m - k), courant > 0.0


def flux_stencil(mass, n, k, w, positive):
    zero = jnp.zeros_like(mass)
    a, b, c = mass * n, mass * k, mass * w
    bp, cp = jnp.where(positive, b, zero), jnp.where(positive, c, zero)
    bm, cm = b - bp, c - cp
    s, t = 7.0 / 12.0, 1.0 / 12.0
    return (
        -t * cp,
        s * cp - t * a,
        s * (a + cp) - t * cm + bp,
        s * (a + cm) - t * cp + bm,
        s * cm - t * a,
        -t * cm,
    )


def divergence_stencil(faces, ahead):
    nxt = [ahead(f) for f in faces]
    return (
        [-faces[0]] + [nxt[i] - faces[i + 1] for i in range(5)] + [nxt[5]]
    )


def meridional(band, hx, cy, e_scr, base, store):
    first = (band * ROWS).astype(F32)
    ids = first + lax.broadcasted_iota(jnp.int32, (16, LANES), 0).astype(F32)
    centre = jnp.sin(math.pi * (ids + 0.5) / NLAT)[:, :1]
    face_cos = jnp.sin(math.pi * ids / NLAT)[:, :1]
    e_scr[0:16] = (7.0 / 12.0) * (hx[1:17] + hx[2:18]) - (1.0 / 12.0) * (hx[0:16] + hx[3:19])
    e_scr[16:24] = jnp.zeros((8, NLON), F32)
    c = cy[...]
    n, k, w, positive = face_coefs(c)
    cell = jnp.where(positive, hx[2:18], hx[3:19])
    far = jnp.where(positive, e_scr[0:16], e_scr[2:18])
    mass = c * face_cos * (n * e_scr[1:17] + k * cell + w * far)
    faces = flux_stencil(mass, n, k, w, positive)

    def ahead(x):
        return pltpu.roll(x, 15, 0)

    stencil = divergence_stencil(faces, ahead)
    per_centre = 1.0 / centre
    new_thick = base - (ahead(mass) - mass) * per_centre
    inverse = 1.0 / new_thick
    scale = inverse * per_centre
    for d in range(7):
        weight = -stencil[d] * scale
        if d == 3:
            weight = weight + hx[3:19] * inverse
        store[d] = weight
    store[7] = -inverse
    return new_thick


def row_of(ref, index, row):
    return jnp.broadcast_to(ref[index, row : row + 1, :], (NT, NLON))


def lane_ids(rows=NT):
    return lax.broadcasted_iota(jnp.int32, (rows, LANES), 1)


def turn(x, amount):
    amount %= LANES
    return x if amount == 0 else pltpu.roll(x, amount, 1)


def window(lanes, low, high, dest):
    if dest == 0:
        return low
    keep = lanes < LANES - TAIL * dest
    return jnp.where(keep, turn(low, -TAIL * dest), turn(high, -TAIL * dest))


def pack_message(rows, ratio_row, new_thick, msg):
    lanes = lane_ids()
    tails = [jnp.zeros((NT, LANES), F32)] * NLEV
    for v, r in enumerate(rows):
        ratio = ratio_row(r)
        part = [ratio[:, LANES * c : LANES * (c + 1)] for c in range(CHUNKS)]
        here = (lanes >= TAIL * v) & (lanes < TAIL * (v + 1))
        for dest in range(NLEV):
            msg[dest, 8 * v : 8 * v + 8, :] = window(lanes, part[dest], part[dest + 1], dest)
            tails[dest] = jnp.where(here, turn(part[dest + 1], TAIL * (v - dest)), tails[dest])
    for dest in range(NLEV):
        msg[dest, 8 * HALF : 8 * HALF + 8, :] = tails[dest]
    lanes16 = lane_ids(16)
    wide = lane_ids(1)
    base = 8 * HALF + 8
    for dest in range(NLEV):
        low = new_thick[:, LANES * dest : LANES * (dest + 1)]
        high = new_thick[:, LANES * (dest + 1) : LANES * (dest + 2)]
        main = window(lanes16, low, high, dest)
        last = jnp.ones((1, LANES), F32)
        for v, r in enumerate(rows):
            msg[dest, base + v : base + v + 1, :] = main[r : r + 1]
            here = (wide >= TAIL * v) & (wide < TAIL * (v + 1))
            last = jnp.where(here, turn(high[r : r + 1], TAIL * (v - dest)), last)
        msg[dest, base + HALF : base + HALF + 1, :] = last
        msg[dest, base + HALF + 1 : base + HALF + 2, :] = jnp.ones((1, LANES), F32)


def tracer_tile(ref, row, chunk):
    return ref[pl.ds(CHUNKS * row + chunk, NT, stride=CHUNKS * ROWS), :]


def put_edge(ref, first, q_ref, h_ref, cy_ref):
    for i in range(HALO):
        for c in range(CHUNKS):
            at = 8 * (CHUNKS * i + c)
            ref[at : at + 8, :] = tracer_tile(q_ref, first + i, c)
    at = 8 * CHUNKS * HALO
    size = CHUNKS * HALO
    for i in range(size):
        ref[at + i : at + i + 1, :] = h_ref[CHUNKS * first + i]
    for i in range(CHUNKS):
        ref[at + size + i : at + size + i + 1, :] = cy_ref[i]
    ref[at + size + CHUNKS : SEND, :] = jnp.zeros((SEND - at - size - CHUNKS, LANES), F32)


def split_bf16(x):
    high = x.astype(BF16)
    return high, (x - high.astype(F32)).astype(BF16)


def dot_parts(x, basis_high, basis_low, dims):
    high, low = split_bf16(x)
    rows = x.shape[0]
    both = lax.dot_general(
        jnp.concatenate([high, low], axis=0), basis_high, dims, preferred_element_type=F32
    )
    small = lax.dot_general(high, basis_low, dims, preferred_element_type=F32)
    return both[:rows] + both[rows:] + small


FORWARD = (((1,), (0,)), ((), ()))
BACKWARD = (((1,), (1,)), ((), ()))


def filter_tables():
    b = np.arange(LANES)
    m = np.arange(LANES)
    blocks = []
    for s in range(1, 5):
        angle = 2.0 * np.pi * ((b[:, None] * (CHUNKS * m[None] + s)) % NLON) / NLON
        cos, sin = np.cos(angle), np.sin(angle)
        blocks.append(np.block([[cos, -sin], [sin, cos]]))
    angle = 2.0 * np.pi * ((b[:, None] * m[None]) % LANES) / LANES
    zero = np.where(m[None] <= LANES // 2, np.cos(angle), np.sin(angle))
    wide = np.stack(blocks)

    def halves(x):
        high = x.astype(np.float32).astype(ml_dtypes.bfloat16)
        low = (x - high.astype(np.float64)).astype(np.float32).astype(ml_dtypes.bfloat16)
        return np.stack([high, low])

    waves = np.concatenate([CHUNKS * m + s for s in range(5)])
    sines = np.sin(np.pi * waves / NLON)
    limit = np.where(waves == 0, 1e30, 4.0 / np.where(waves == 0, 1.0, sines * sines))
    weight = np.full(waves.shape, 2.0 / NLON)
    weight[0] = 1.0 / NLON
    weight[LANES // 2] = 1.0 / NLON
    table = np.zeros((8, waves.size), np.float32)
    table[0], table[1] = limit, weight
    return halves(wide), halves(zero), table


def smooth(band, rows, z_scr, spec_scr, wide_ref, zero_ref, table_ref):
    first = (band * ROWS).astype(F32)
    ids = first + lax.broadcasted_iota(jnp.int32, (16, LANES), 0).astype(F32)
    centre = jnp.sin(math.pi * (ids + 0.5) / NLAT)[:, :1]
    damping = jnp.minimum(1.0, centre * centre * table_ref[0:1, :]) * table_ref[1:2, :]
    x = [z_scr[:, LANES * a : LANES * (a + 1)] for a in range(CHUNKS)]
    plus = [x[a] + x[CHUNKS - a] for a in range(1, 5)]
    minus = [x[a] - x[CHUNKS - a] for a in range(1, 5)]

    def damp(block):
        blocks = [
            jnp.broadcast_to(damping[r : r + 1, LANES * block : LANES * (block + 1)], (NT, LANES))
            for r in rows
        ]
        return jnp.concatenate(blocks, axis=0)

    total = x[0] + plus[0] + plus[1] + plus[2] + plus[3]
    spectrum = dot_parts(total, zero_ref[0], zero_ref[1], FORWARD) * damp(0)
    spec_scr[:, 0:LANES] = dot_parts(spectrum, zero_ref[0], zero_ref[1], BACKWARD)
    for s in range(1, 5):
        real, imag = x[0], None
        for a in range(1, 5):
            angle = 2.0 * math.pi * (s * a % CHUNKS) / CHUNKS
            real = real + plus[a - 1] * math.cos(angle)
            term = minus[a - 1] * -math.sin(angle)
            imag = term if imag is None else imag + term
        spectrum = dot_parts(
            jnp.concatenate([real, imag], axis=1), wide_ref[0, s - 1], wide_ref[1, s - 1], FORWARD
        )
        factor = damp(s)
        spectrum = spectrum * jnp.concatenate([factor, factor], axis=1)
        at = LANES * (2 * s - 1)
        spec_scr[:, at : at + 2 * LANES] = dot_parts(
            spectrum, wide_ref[0, s - 1], wide_ref[1, s - 1], BACKWARD
        )
    mean = spec_scr[:, 0:LANES]
    real = [spec_scr[:, LANES * (2 * s - 1) : LANES * 2 * s] for s in range(1, 5)]
    imag = [spec_scr[:, LANES * 2 * s : LANES * (2 * s + 1)] for s in range(1, 5)]
    z_scr[:, 0:LANES] = mean + real[0] + real[1] + real[2] + real[3]
    for a in range(1, 5):
        even, odd = mean, None
        for s in range(1, 5):
            angle = 2.0 * math.pi * (s * a % CHUNKS) / CHUNKS
            even = even + real[s - 1] * math.cos(angle)
            term = imag[s - 1] * math.sin(angle)
            odd = term if odd is None else odd + term
        z_scr[:, LANES * a : LANES * (a + 1)] = even - odd
        b = CHUNKS - a
        z_scr[:, LANES * b : LANES * (b + 1)] = even + odd


def combine(r, weights, q_of, z_row):
    total = row_of(weights, 7, r) * z_row
    for d in range(7):
        total = total + row_of(weights, d, r) * q_of(r + d - HALO)
    return total


def spread(ref, scr, at):
    for r in range(ROWS):
        for c in range(CHUNKS):
            scr[at + r : at + r + 1, LANES * c : LANES * (c + 1)] = ref[CHUNKS * r + c]


def is_polar(band):
    south, north = band * ROWS, NLAT - 1 - (band * ROWS + ROWS - 1)
    return jnp.minimum(south, north) < NLAT // 6


def zonal(rows, q_in, h_in, cx_in, cx_scr, hx_scr, wx_scr, z_scr, smooth_rows):
    band = lax.axis_index("lat")
    hx_scr[...] = jnp.zeros(hx_scr.shape, F32)
    spread(h_in, hx_scr, HALO)
    spread(cx_in, cx_scr, 0)
    cx_scr[ROWS:16] = jnp.zeros((4, NLON), F32)
    h = hx_scr[HALO : HALO + 16]
    c = cx_scr[...]
    n, k, w, positive = face_coefs(c)
    west = shifted(h, -1)
    edge = (7.0 / 12.0) * (west + h) - (1.0 / 12.0) * (shifted(h, -2) + shifted(h, 1))
    far = jnp.where(positive, shifted(edge, -1), shifted(edge, 1))
    mass = c * (n * edge + k * jnp.where(positive, west, h) + w * far)
    faces = flux_stencil(mass, n, k, w, positive)
    stencil = divergence_stencil(faces, lambda f: shifted(f, 1))
    for d in range(7):
        wx_scr[d] = stencil[d]
    for v, r in enumerate(rows):
        row = tracer_row(q_in, r)
        total = row_of(wx_scr, 3, r) * row
        for d in (-3, -2, -1, 1, 2, 3):
            total = total + row_of(wx_scr, d + 3, r) * shifted(row, d)
        z_scr[NT * v : NT * (v + 1), :] = total

    @pl.when(is_polar(band))
    def _():
        smooth_rows(band)

    return h - (shifted(mass, 1) - mass)


def tracer_row(ref, row):
    return jnp.concatenate([tracer_tile(ref, row, chunk) for chunk in range(CHUNKS)], axis=1)


def is_early(band):
    return band % 4 < 2


def inner_work(band, far_refs, near_refs, msg_far, work, semaphores, loaded):
    msg, cx_scr, hx_scr, cy_scr, e_scr, wx_scr, wy_scr, z_scr, spec_scr, q_scr = work
    q_in, h_in, cy_in, cx_in, wide_ref, zero_ref, table_ref = near_refs
    loads = [
        pltpu.make_async_copy(far_refs[i], near_refs[i], semaphores.at[i]) for i in range(loaded, 7)
    ]
    fields, tables = loads[: 4 - loaded], loads[4 - loaded :]
    for load in fields:
        load.start()

    @pl.when(is_polar(band))
    def _():
        for load in tables:
            load.start()

    for load in fields:
        load.wait()

    def smooth_rows(band):
        for load in tables:
            load.wait()
        smooth(band, INNER, z_scr, spec_scr, wide_ref, zero_ref, table_ref)

    base = zonal(INNER, q_in, h_in, cx_in, cx_scr, hx_scr, wx_scr, z_scr, smooth_rows)
    spread(cy_in, cy_scr, 0)
    cy_scr[ROWS:16] = jnp.zeros((4, NLON), F32)
    new_thick = meridional(band, hx_scr, cy_scr, e_scr, base, wy_scr)
    for r in range(ROWS):
        q_scr[r] = tracer_row(q_in, r)

    def ratio_row(r):
        v = INNER.index(r)
        return combine(r, wy_scr, lambda j: q_scr[j], z_scr[NT * v : NT * (v + 1), :])

    pack_message(INNER, ratio_row, new_thick, msg)
    move = pltpu.make_async_copy(msg, msg_far, semaphores.at[7])
    move.start()
    move.wait()


def edge_kernel(*refs):
    far_refs, (odd_ref, even_ref, msg_far), near_refs = refs[:7], refs[7:10], refs[10:17]
    work, semaphores = refs[17:27], refs[27]
    q_ref, h_ref, cy_ref = near_refs[:3]
    band = lax.axis_index("lat")
    loads = copies(semaphores, *zip(far_refs[:3], near_refs[:3]))
    for load in loads:
        load.start()
    for load in loads:
        load.wait()

    @pl.when(band % 2 == 0)
    def _():
        put_edge(even_ref, ROWS - HALO, q_ref, h_ref, cy_ref)
        put_edge(odd_ref, 0, q_ref, h_ref, cy_ref)

    @pl.when(band % 2 == 1)
    def _():
        put_edge(odd_ref, ROWS - HALO, q_ref, h_ref, cy_ref)
        put_edge(even_ref, 0, q_ref, h_ref, cy_ref)

    @pl.when(is_early(band))
    def _():
        inner_work(band, far_refs, near_refs, msg_far, work, semaphores, 3)


def inner_kernel(*refs):
    far_refs, msg_far, near_refs = refs[:7], refs[10], refs[11:18]
    work, semaphores = refs[18:28], refs[28]
    band = lax.axis_index("lat")

    @pl.when(jnp.logical_not(is_early(band)))
    def _():
        inner_work(band, far_refs, near_refs, msg_far, work, semaphores, 0)


def zonal_kernel(
    q_in, h_in, cx_in, wide_ref, zero_ref, table_ref,
    z_out, base_out,
    cx_scr, hx_scr, wx_scr, spec_scr,
):
    def smooth_rows(band):
        smooth(band, OUTER, z_out, spec_scr, wide_ref, zero_ref, table_ref)

    base_out[...] = zonal(OUTER, q_in, h_in, cx_in, cx_scr, hx_scr, wx_scr, z_out, smooth_rows)


def outer_kernel(
    q_in, z_ref, base_ref, h_in, cy_in, odd_ref, even_ref,
    msg,
    hx_scr, cy_scr, e_scr, wy_scr, q_scr,
):
    band = lax.axis_index("lat")
    spread(h_in, hx_scr, HALO)
    hx_scr[ROWS + 2 * HALO : 24] = jnp.zeros((24 - ROWS - 2 * HALO, NLON), F32)
    spread(cy_in, cy_scr, 0)
    cy_scr[ROWS:16] = jnp.zeros((4, NLON), F32)

    def take(south_ref, north_ref):
        for i in range(HALO):
            for c in range(CHUNKS):
                at = 8 * (CHUNKS * i + c)
                lanes = slice(LANES * c, LANES * (c + 1))
                q_scr[i, :, lanes] = south_ref[at : at + 8, :]
                q_scr[HALO + ROWS + i, :, lanes] = north_ref[at : at + 8, :]
        for c in range(CHUNKS):
            at = 8 * CHUNKS * HALO + c
            lanes = slice(LANES * c, LANES * (c + 1))
            hx_scr[0:HALO, lanes] = south_ref[pl.ds(at, HALO, stride=CHUNKS), :]
            hx_scr[HALO + ROWS : ROWS + 2 * HALO, lanes] = north_ref[pl.ds(at, HALO, stride=CHUNKS), :]
            at = at + CHUNKS * HALO
            cy_scr[ROWS : ROWS + 1, lanes] = north_ref[at : at + 1, :]

    @pl.when(band % 2 == 0)
    def _():
        take(odd_ref, even_ref)

    @pl.when(band % 2 == 1)
    def _():
        take(even_ref, odd_ref)

    new_thick = meridional(band, hx_scr, cy_scr, e_scr, base_ref[...], wy_scr)

    for r in range(ROWS):
        q_scr[HALO + r] = tracer_row(q_in, r)

    def ratio_row(r):
        v = OUTER.index(r)
        return combine(r, wy_scr, lambda j: q_scr[HALO + j], z_ref[NT * v : NT * (v + 1), :])

    pack_message(OUTER, ratio_row, new_thick, msg)


def remap_kernel(weight_ref, first_ref, second_ref, out_ref, mass_ref, inter_scr):
    weight_sum = weight_ref[0]
    for k in range(1, NLEV):
        weight_sum = weight_sum + weight_ref[k]
    base = 8 * HALF + 8
    for in_ref, rows in ((first_ref, INNER), (second_ref, OUTER)):
        thick = [in_ref[i, base : base + 8, :] for i in range(NLEV)]
        upper, lower = [thick[0]], []
        for i in range(1, NLEV):
            upper.append(upper[-1] + thick[i])
        for i in range(NLEV):
            lower.append(upper[i] - thick[i])
        total = upper[-1]
        for v, r in enumerate(rows):
            mass_ref[r : r + 1, 0:LANES] = total[v : v + 1]
            mass_ref[r : r + 1, LANES:PIECE] = turn(total[HALF : HALF + 1], -TAIL * v)[:, :TAIL]
        reach = None
        for k in range(NLEV):
            target = total * (weight_ref[k] / weight_sum)
            reach = target if reach is None else reach + target
            start = reach - target
            scale = 1.0 / target
            for i in range(NLEV):
                overlap = jnp.minimum(upper[i], reach) - jnp.maximum(lower[i], start)
                at = 8 * (NLEV * i + k)
                inter_scr[at : at + 8, :] = jnp.maximum(overlap, 0.0) * scale
        for v in range(HALF + 1):
            moved = [None] * NT
            for i in range(NLEV):
                share = inter_scr[pl.ds(8 * NLEV * i + v, NLEV, stride=8), :]
                for t in range(NT):
                    at = 8 * v + t
                    term = jnp.broadcast_to(in_ref[i, at : at + 1, :], (NLEV, LANES)) * share
                    moved[t] = term if i == 0 else moved[t] + term
            for t in range(NT):
                if v < HALF:
                    out_ref[t, rows[v], :, 0:LANES] = moved[t]
                else:
                    for u, r in enumerate(rows):
                        out_ref[t, r, :, LANES:PIECE] = turn(moved[t], -TAIL * u)[:, :TAIL]


def swaps(first, bands):
    low = range(first, bands - 1, 2)
    return [(i, i + 1) for i in low] + [(i + 1, i) for i in low]


def shape(*dims):
    return jax.ShapeDtypeStruct(dims, F32)


def scratch(*dims):
    return pltpu.VMEM(dims, F32)


def local(tracers, thickness, courant_x, courant_y, level_weights):
    bands = lax.axis_size("lat")
    wide, zero, table = filter_tables()
    q_in = tracers.reshape(NT * ROWS * CHUNKS, LANES)
    h_in, cx_in, cy_in = (
        field.reshape(ROWS * CHUNKS, 1, LANES) for field in (thickness, courant_x, courant_y)
    )
    tables = tuple(jnp.asarray(t) for t in (wide, zero, table))
    operands = (q_in, h_in, cy_in, cx_in, *tables)
    room = (
        [scratch(NT * ROWS * CHUNKS, LANES)]
        + [scratch(ROWS * CHUNKS, 1, LANES)] * 3
        + [pltpu.VMEM(t.shape, t.dtype) for t in tables]
        + [
            scratch(NLEV, MSG, LANES),
            scratch(16, NLON), scratch(24, NLON), scratch(16, NLON), scratch(24, NLON),
            scratch(7, 16, NLON), scratch(8, 16, NLON),
            scratch(HALF * NT, NLON), scratch(HALF * NT, NLON), scratch(ROWS, NT, NLON),
            pltpu.SemaphoreType.DMA((8,)),
        ]
    )
    odd, even, message = pl.pallas_call(
        edge_kernel,
        out_shape=(shape(SEND, LANES),) * 2 + (shape(NLEV, MSG, LANES),),
        in_specs=[far()] * 7,
        out_specs=(vmem(),) * 2 + (far(),),
        scratch_shapes=room,
        compiler_params=params(WHOLE),
        name="edge_rows",
    )(*operands)
    sent = (odd, even)
    odd = lax.ppermute(odd, "lat", swaps(1, bands))
    even = lax.ppermute(even, "lat", swaps(0, bands))
    message = pl.pallas_call(
        inner_kernel,
        out_shape=shape(NLEV, MSG, LANES),
        in_specs=[far()] * 10,
        out_specs=far(),
        scratch_shapes=room,
        input_output_aliases={7: 0},
        compiler_params=params(WHOLE),
        name="inner_rows",
    )(*operands, message, *sent)
    first = message
    first = lax.all_to_all(first, "lev", split_axis=0, concat_axis=0, tiled=True)
    z, base = pl.pallas_call(
        zonal_kernel,
        out_shape=(shape(HALF * NT, NLON), shape(16, NLON)),
        in_specs=[vmem()] * 6,
        out_specs=(vmem(),) * 2,
        scratch_shapes=[
            scratch(16, NLON), scratch(24, NLON), scratch(7, 16, NLON), scratch(HALF * NT, NLON),
        ],
        compiler_params=params(32),
        cost_estimate=pl.CostEstimate(flops=ZFLOPS, bytes_accessed=ZBYTES, transcendentals=0),
        name="outer_zonal",
    )(q_in, h_in, cx_in, *tables)
    second = pl.pallas_call(
        outer_kernel,
        out_shape=shape(NLEV, MSG, LANES),
        in_specs=[vmem()] * 7,
        out_specs=vmem(),
        scratch_shapes=[
            scratch(24, NLON), scratch(16, NLON), scratch(24, NLON), scratch(8, 16, NLON),
            scratch(ROWS + 2 * HALO, NT, NLON),
        ],
        compiler_params=params(32),
        name="outer_rows",
    )(q_in, z, base, h_in, cy_in, odd, even)
    second = lax.all_to_all(second, "lev", split_axis=0, concat_axis=0, tiled=True)
    remapped, column_mass = pl.pallas_call(
        remap_kernel,
        out_shape=(shape(NT, ROWS, NLEV, PIECE), shape(ROWS, PIECE)),
        in_specs=[pl.BlockSpec(memory_space=pltpu.SMEM), vmem(), vmem()],
        out_specs=(vmem(),) * 2,
        scratch_shapes=[scratch(NLEV * NLEV * 8, LANES)],
        compiler_params=params(32),
        name="remap",
    )(level_weights, first, second)
    return jnp.transpose(remapped, (0, 2, 1, 3)), column_mass


def solution(mesh):
    placed = (
        P(None, "lev", "lat", None),
        P("lev", "lat", None),
        P("lev", "lat", None),
        P("lev", "lat", None),
        P(),
    )
    return jax.shard_map(
        local,
        mesh=mesh,
        in_specs=placed,
        out_specs=(P(None, None, "lat", "lev"), P("lat", "lev")),
        check_vma=False,
    )
```
